512 devices in a mesh: row: 16 (over z), col: 16 (over y_hi, x, core), rep: 2 (over y_lo).
Axes of the slice: x: 4, y: 4 (y_hi: 2, y_lo: 2; y = y_hi * 2 + y_lo), z: 16, core: 2. Of those that a mesh axis runs over, the one named last changes fastest.
Arguments:
- pair_rep: bfloat16 [1024, 1024, 128], P(('row', 'rep'), 'col'), may hold values from -6 to 6
- token_mask: int32 [1024], replicated, may hold values 0 or 1
- w_a: bfloat16 [128, 128], replicated, may hold values from -0.5 to 0.5
- w_a_gate: bfloat16 [128, 128], replicated, may hold values from -0.5 to 0.5
- w_b: bfloat16 [128, 128], replicated, may hold values from -0.5 to 0.5
- w_b_gate: bfloat16 [128, 128], replicated, may hold values from -0.5 to 0.5
- w_gate: bfloat16 [128, 128], replicated, may hold values from -0.5 to 0.5
- w_out: bfloat16 [128, 128], replicated, may hold values from -0.5 to 0.5
Outputs:
- update: bfloat16 [1024, 1024, 128], P(('row', 'rep'), 'col')
The draws below stay inside these ranges and needn't reach their ends.
All inputs are finite; a program needn't handle non-finite values.
Results may differ from the reference program's by a relative error of at most 0.018.
Values may be sent and summed in bfloat16 or wider, within the bound.
No kernel may reach another device: no remote copies, remote signals or barrier semaphores. Data moves between devices by JAX's collectives and lax.ppermute only.
A program may use at most 64 MiB of HBM per device.

```python
import jax
import jax.numpy as jnp
from jax import lax

C = 128
HID = 128
TILE = 64
STEPS = 2
N = 1024


def place_ends(entries, rng, least, top_value):
    longest = entries.shape.index(max(entries.shape))
    spots = []
    for shift in (0, 1):
        where = [jax.random.randint(jax.random.fold_in(rng, axis), (), 0, length) for axis, length in enumerate(entries.shape)]
        where[longest] = (where[longest] + shift) % entries.shape[longest]
        spots.append(tuple(where))
    return entries.at[spots[0]].set(least).at[spots[1]].set(top_value)


def levels(stream_key, shape, split, smallest, largest):
    loudness = 1.0
    for position, parts in split:
        draws = jax.random.uniform(jax.random.fold_in(jax.random.fold_in(stream_key, 6), position), (parts,), jnp.float32, smallest / len(split), largest / len(split))
        loudness = loudness * jnp.repeat(jnp.exp(draws), shape[position] // parts).reshape((-1,) + (1,) * (len(shape) - 1 - position))
    return loudness


def gaussian(rng, extent, scale, bound, cuts=(), kind=jnp.bfloat16):
    factor_of = levels(rng, extent, cuts, -0.22, 0.18) if cuts else 1.0
    result = jax.random.normal(rng, extent, jnp.float32) * scale * factor_of
    return jnp.minimum(jnp.maximum(result, -bound), bound).astype(kind)


def setup_inputs(seed: int = 0) -> dict:
    seeds = jax.random.split(jax.random.key(seed), 9)
    return {
        "pair_rep": gaussian(seeds[0], (N, N, C), 1.0, 6.0, ((0, 32), (1, 16))),
        "token_mask": place_ends((jax.random.randint(seeds[1], (N,), 0, 8) < 7).astype(jnp.int32), jax.random.fold_in(seeds[1], 1), 0, 1),
        "w_a": gaussian(seeds[2], (C, HID), C ** -0.5, 0.5),
        "w_a_gate": gaussian(seeds[3], (C, HID), C ** -0.5, 0.5),
        "w_b": gaussian(seeds[4], (C, HID), C ** -0.5, 0.5),
        "w_b_gate": gaussian(seeds[5], (C, HID), C ** -0.5, 0.5),
        "w_gate": gaussian(seeds[6], (C, C), C ** -0.5, 0.5),
        "w_out": gaussian(seeds[7], (HID, C), HID ** -0.5, 0.5),
    }


EPS = 1e-05

def layer_norm(values):
    mean = lax.optimization_barrier(jnp.mean(values, axis=-1, keepdims=True))
    centred = values - mean
    var = lax.optimization_barrier(jnp.mean(centred * centred, axis=-1, keepdims=True))
    return centred * lax.rsqrt(var + EPS)

def reference(pair_rep, token_mask, w_a, w_a_gate, w_b, w_b_gate, w_gate, w_out):
    blocks = N // TILE
    maskf = token_mask.astype(jnp.float32)

    def make_rows(index):
        start = (index * TILE).astype(jnp.int32)
        rows = lax.dynamic_slice_in_dim(pair_rep, start, TILE, 0)
        normed = layer_norm(rows.astype(jnp.float32)).astype(jnp.bfloat16)
        mask_rows = lax.dynamic_slice_in_dim(maskf, start, TILE, 0)
        pair = (mask_rows[:, None] * maskf[None, :]).reshape(-1, 1)
        flat = normed.reshape(TILE * N, C)

        def gated(w_value, w_sig):
            value = jnp.dot(flat, w_value, preferred_element_type=jnp.float32)
            sig = jnp.dot(flat, w_sig, preferred_element_type=jnp.float32)
            return (pair * jax.nn.sigmoid(sig) * value).astype(jnp.bfloat16).reshape(TILE, N, HID)
        return (gated(w_a, w_a_gate), gated(w_b, w_b_gate))
    a_rows, b_rows = lax.map(make_rows, jnp.arange(blocks, dtype=jnp.int32))
    left = a_rows.reshape(N, N, HID)
    right = b_rows.reshape(N, N, HID)

    def make_column(index):
        start = (index * TILE).astype(jnp.int32)
        total = jnp.zeros((N, TILE, HID), jnp.float32)
        for step in range(STEPS):
            kstart = ((index + step) % blocks * TILE).astype(jnp.int32)
            a_part = lax.dynamic_slice_in_dim(left, kstart, TILE, 1)
            b_part = lax.dynamic_slice(right, (start, kstart, jnp.int32(0)), (TILE, TILE, HID))
            total = total + jnp.einsum('ikc,jkc->ijc', a_part.astype(jnp.float32), b_part.astype(jnp.float32))
        mean = lax.optimization_barrier(jnp.mean(total, axis=-1, keepdims=True))
        var = lax.optimization_barrier(jnp.mean(total * total, axis=-1, keepdims=True)) - mean * mean
        tri_normed = ((total - mean) * lax.rsqrt(var + EPS)).astype(jnp.bfloat16)
        projected = jnp.dot(tri_normed.reshape(-1, HID), w_out, preferred_element_type=jnp.float32)
        cols = lax.dynamic_slice_in_dim(pair_rep, start, TILE, 1)
        normed = layer_norm(cols.astype(jnp.float32)).astype(jnp.bfloat16)
        gate = jax.nn.sigmoid(jnp.dot(normed.reshape(-1, C), w_gate, preferred_element_type=jnp.float32))
        return (gate * projected).astype(jnp.bfloat16).reshape(N, TILE, C)
    columns = lax.map(make_column, jnp.arange(blocks, dtype=jnp.int32))
    return jnp.transpose(columns, (1, 0, 2, 3)).reshape(N, N, C)
```

```python
import jax
import jax.numpy as jnp
from jax import lax
from jax.sharding import PartitionSpec as P

HID = 128
EPS = 1e-05


def layer_norm(values):
    mean = jnp.mean(values, axis=-1, keepdims=True)
    centred = values - mean
    var = jnp.mean(centred * centred, axis=-1, keepdims=True)
    return centred * lax.rsqrt(var + EPS)


def project(values, weights):
    return jnp.dot(values, weights, preferred_element_type=jnp.float32)


def gated(normed, w_value, w_sig, pair):
    return (pair * jax.nn.sigmoid(project(normed, w_sig)) * project(normed, w_value)).astype(jnp.bfloat16)


def tri_projected(left, right, w_out):
    tri = jnp.einsum("ikc,jkc->ijc", left, right, preferred_element_type=jnp.float32)
    mean = jnp.mean(tri, axis=-1, keepdims=True)
    var = jnp.mean(tri * tri, axis=-1, keepdims=True) - mean * mean
    normed = ((tri - mean) * lax.rsqrt(var + EPS)).astype(jnp.bfloat16)
    return project(normed, w_out)


def per_device(pair_rep, token_mask, w_a, w_a_gate, w_b, w_b_gate, w_gate, w_out):
    half, tile, chans = pair_rep.shape
    rows, cols, reps = lax.axis_size("row"), lax.axis_size("col"), lax.axis_size("rep")
    row, col, rep = lax.axis_index("row"), lax.axis_index("col"), lax.axis_index("rep")
    maskf = token_mask.astype(jnp.float32)
    mask_i = lax.dynamic_slice_in_dim(maskf, row * tile + rep * half, half, 0)
    mask_k = lax.dynamic_slice_in_dim(maskf, col * tile, tile, 0)
    pair = (mask_i[:, None] * mask_k[None, :]).reshape(-1, 1)
    normed = layer_norm(pair_rep.astype(jnp.float32)).astype(jnp.bfloat16).reshape(-1, chans)

    right = gated(normed, w_b, w_b_gate, pair)
    sends = rows // 2
    kept = right.shape[0] // rows * (rows - 1)
    piece = kept // sends
    rest = right[kept:]
    mine = None
    for s in range(sends):
        pairs = [(c * cols + c, 2 * s * cols + c) for c in range(cols)]
        pairs += [(c * cols + (c + 1) % cols, (2 * s + 1) * cols + c) for c in range(cols)]
        message = jnp.concatenate([right[s * piece : (s + 1) * piece], rest])
        got = lax.ppermute(message, ("row", "col"), pairs)
        mine = got if mine is None else mine + got

    left = gated(normed, w_a, w_a_gate, pair)
    swap = [(p, 1 - p) for p in range(reps)]
    back = [(c, (c - 1) % cols) for c in range(cols)]
    left_next = lax.ppermute(left, "col", back)
    other = lax.ppermute(left, "rep", swap)
    other_next = lax.ppermute(left_next, "rep", swap)

    rest_mine = mine[piece:]
    rest_other = lax.ppermute(rest_mine, "row", [(r, r ^ 1) for r in range(rows)])
    gathered = lax.all_gather(mine[:piece], "row", axis=0, tiled=True)
    gathered = gathered.reshape(sends, 2, piece, chans)
    even = row % 2 == 0
    rests = (jnp.where(even, rest_mine, rest_other), jnp.where(even, rest_other, rest_mine))
    right_all = jnp.concatenate(
        [
            jnp.concatenate([gathered[:, t].reshape(-1, chans), rests[t]]).reshape(half, tile, chans)
            for t in range(2)
        ],
        axis=1,
    )

    def both(first, second):
        return jnp.concatenate([first.reshape(half, tile, chans), second.reshape(half, tile, chans)], axis=1)

    theirs = tri_projected(both(other, other_next), right_all, w_out).astype(jnp.bfloat16)
    received = lax.ppermute(theirs, "rep", swap)
    ours = tri_projected(both(left, left_next), right_all, w_out)
    gate = jax.nn.sigmoid(project(normed, w_gate)).reshape(half, tile, chans)
    ours, received = ours.reshape(half, half, chans), received.reshape(half, half, chans).astype(jnp.float32)
    first = rep == 0
    projected = jnp.concatenate([jnp.where(first, ours, received), jnp.where(first, received, ours)], axis=1)
    return (gate * projected).astype(jnp.bfloat16)


def solution(mesh):
    placed = (P(("row", "rep"), "col", None), P(), P(), P(), P(), P(), P(), P())
    return jax.shard_map(
        per_device,
        mesh=mesh,
        in_specs=placed,
        out_specs=P(("row", "rep"), "col", None),
        check_vma=False,
    )
```

```python
import functools
import jax
import jax.numpy as jnp
from jax import lax
from jax.experimental import pallas as pl
from jax.experimental.pallas import tpu as pltpu
from jax.sharding import PartitionSpec as P

EPS = 1e-5
VMEM = pl.BlockSpec(memory_space=pltpu.VMEM)
SMEM = pl.BlockSpec(memory_space=pltpu.SMEM)
F32 = jnp.float32
BF16 = jnp.bfloat16

def row_sums(values, ones):
    return lax.dot_general(values, ones, (((1,), (0,)), ((), ())), preferred_element_type=F32)

def normalise(block, ones):
    chans = block.shape[1]
    centred = block.astype(F32) - row_sums(block, ones) * (1.0 / chans)
    squares = centred * centred
    high = squares.astype(BF16)
    low = (squares - high.astype(F32)).astype(BF16)
    var = (row_sums(high, ones) + row_sums(low, ones)) * (1.0 / chans)
    return (centred * lax.rsqrt(var + EPS)).astype(BF16)

def dot_t(a, b):
    return lax.dot_general(a, b, (((1,), (1,)), ((), ())), preferred_element_type=F32)

def transposed(w):
    return w[...].astype(F32).T.astype(BF16)

def gated(weights, normed, mask):
    both = dot_t(weights, normed)
    c = both.shape[0] // 2
    return both[:c] * mask * jax.nn.sigmoid(both[c:])

def left_kernel(flags, x, x_next, mask_k, w, w_gate, out, wt, held):
    half, tile, chans = x.shape
    hid = w.shape[1]
    wt[:hid] = transposed(w)
    wt[hid:] = transposed(w_gate)
    ones = jnp.ones((chans, chans), BF16)
    weights = wt[...]
    def step(i, carry):
        block = jnp.concatenate([x[i], x_next[i]], axis=0)
        got = gated(weights, normalise(block, ones), mask_k[...] * flags[i].astype(F32))
        held[pl.ds(i, hid, stride=half), :] = got
        return carry
    lax.fori_loop(0, half, step, 0, unroll=4)
    def cast(c, carry):
        out[pl.ds(c * 8, 8)] = held[pl.ds(pl.multiple_of(c * 8 * half, 8 * half), 8 * half), :].reshape(8, half, 2 * tile).astype(BF16)
        return carry
    lax.fori_loop(0, hid // 8, cast, 0)

def left_call(flags, x, x_next, mask_k, w, w_gate):
    half, tile, chans = x.shape
    hid = w.shape[1]
    return pl.pallas_call(
        left_kernel,
        out_shape=jax.ShapeDtypeStruct((hid, half, 2 * tile), BF16),
        in_specs=[SMEM] + [VMEM] * 5,
        out_specs=VMEM,
        scratch_shapes=[pltpu.VMEM((2 * hid, chans), BF16), pltpu.VMEM((hid * half, 2 * tile), F32)],
        compiler_params=pltpu.CompilerParams(vmem_limit_bytes=32 << 20),
        name="left",
        cost_estimate=pl.CostEstimate(flops=2*half*tile*2*chans*5*hid, bytes_accessed=4 << 20, transcendentals=half*tile*2*hid*2),
    )(flags, x, x_next, mask_k, w, w_gate)

def chunk_kernel(piece, *refs):
    *got, out, rest = refs
    chans = out.shape[1]
    total = got[0][...]
    for g in got[1:]:
        total = total + g[...]
    normed = normalise(total, jnp.ones((chans, chans), BF16))
    out[...] = normed[:piece]
    rest[...] = normed[piece:]

def chunk_call(got, piece):
    n, chans = got[0].shape
    return pl.pallas_call(
        functools.partial(chunk_kernel, piece),
        out_shape=(jax.ShapeDtypeStruct((piece, chans), BF16), jax.ShapeDtypeStruct((n - piece, chans), BF16)),
        in_specs=[VMEM] * len(got),
        out_specs=(VMEM, VMEM),
        compiler_params=pltpu.CompilerParams(vmem_limit_bytes=16 << 20),
        name="chunk",
        cost_estimate=pl.CostEstimate(flops=0, bytes_accessed=1 << 20, transcendentals=0),
    )(*got)

def tri_project(left, right, w_out, held, half):
    hid = left.shape[0]
    group = 8
    def channel(g, carry):
        for u in range(group):
            c = g * group + u
            held[pl.ds(c, half, stride=hid), :half] = dot_t(left[c], right[c])
        return carry
    lax.fori_loop(0, hid // group, channel, 0)
    weights = w_out[...]
    def projected(i):
        tri = held[pl.ds(pl.multiple_of(i * hid, hid), hid), :half]
        mean = jnp.sum(tri, axis=0, keepdims=True) * (1.0 / hid)
        var = jnp.sum(tri * tri, axis=0, keepdims=True) * (1.0 / hid) - mean * mean
        normed = ((tri - mean) * lax.rsqrt(var + EPS)).astype(BF16)
        return lax.dot_general(normed, weights, (((0,), (0,)), ((), ())), preferred_element_type=F32)
    return projected

def right_kernel(order, flags, gathered, rest_a, rest_b, mask_k, w, w_gate, left, w_out, out, right, wt, tiles, held, tri):
    shards, piece, chans = gathered.shape
    hid, half, width = left.shape
    tile = width // 2
    kept = shards // 2 * piece
    wt[:hid] = transposed(w)
    wt[hid:] = transposed(w_gate)
    for s in range(shards // 2):
        for t in range(2):
            tiles[t, pl.ds(s * piece, piece)] = gathered[order[2 * s + t]]
    tiles[0, kept:] = rest_a[...]
    tiles[1, kept:] = rest_b[...]
    weights = wt[...]
    def step(j, carry):
        at = pl.ds(pl.multiple_of(j * tile, tile), tile)
        block = jnp.concatenate([tiles[0, at], tiles[1, at]], axis=0)
        held[pl.ds(j, hid, stride=half), :] = gated(weights, block, mask_k[...] * flags[j].astype(F32))
        return carry
    lax.fori_loop(0, half, step, 0, unroll=4)
    def cast(c, carry):
        right[pl.ds(c * 8, 8)] = held[pl.ds(pl.multiple_of(c * 8 * half, 8 * half), 8 * half), :].reshape(8, half, width).astype(BF16)
        return carry
    lax.fori_loop(0, hid // 8, cast, 0)
    projected = tri_project(left, right, w_out, tri, half)
    def row(i, carry):
        out[i] = projected(i).astype(BF16)
        return carry
    lax.fori_loop(0, half, row, 0, unroll=4)

def right_call(order, flags, gathered, rest_a, rest_b, mask_k, w, w_gate, left, w_out):
    hid, half, width = left.shape
    chans = gathered.shape[-1]
    return pl.pallas_call(
        right_kernel,
        out_shape=(jax.ShapeDtypeStruct((half, half, chans), BF16), jax.ShapeDtypeStruct((hid, half, width), BF16)),
        in_specs=[SMEM] * 2 + [VMEM] * 8,
        out_specs=(VMEM, VMEM),
        scratch_shapes=[
            pltpu.VMEM((2 * hid, chans), BF16),
            pltpu.VMEM((2, half * width // 2, chans), BF16),
            pltpu.VMEM((hid * half, width), F32),
            pltpu.VMEM((hid * half, 128), F32),
        ],
        compiler_params=pltpu.CompilerParams(vmem_limit_bytes=40 << 20),
        name="right_tri",
        cost_estimate=pl.CostEstimate(flops=2*half*width*chans*2*hid, bytes_accessed=4 << 20, transcendentals=half*width*hid*2),
    )(order, flags, gathered, rest_a, rest_b, mask_k, w, w_gate, left, w_out)

def own_kernel(x, w_gate, left, right, w_out, out, gate, tri):
    half, tile, chans = x.shape
    projected = tri_project(left, right, w_out, tri, half)
    ones = jnp.ones((chans, chans), BF16)
    weights = w_gate[...]
    def row(i, carry):
        out[i] = projected(i)
        gate[i] = jax.nn.sigmoid(jnp.dot(normalise(x[i], ones), weights, preferred_element_type=F32))
        return carry
    lax.fori_loop(0, half, row, 0, unroll=4)

def own_call(x, w_gate, left, right, w_out):
    half, tile, chans = x.shape
    hid = left.shape[0]
    return pl.pallas_call(
        own_kernel,
        out_shape=(jax.ShapeDtypeStruct((half, half, chans), F32), jax.ShapeDtypeStruct((half, tile, chans), F32)),
        in_specs=[VMEM] * 5,
        out_specs=(VMEM, VMEM),
        scratch_shapes=[pltpu.VMEM((hid * half, 128), F32)],
        compiler_params=pltpu.CompilerParams(vmem_limit_bytes=32 << 20),
        name="own_tri",
        cost_estimate=pl.CostEstimate(flops=2*half*tile*chans*chans*4, bytes_accessed=4 << 20, transcendentals=half*tile*chans*2),
    )(x, w_gate, left, right, w_out)


def per_device(pair_rep, token_mask, w_a, w_a_gate, w_b, w_b_gate, w_gate, w_out):
    half, tile, chans = pair_rep.shape
    rows, cols, reps = lax.axis_size("row"), lax.axis_size("col"), lax.axis_size("rep")
    row, col, rep = lax.axis_index("row"), lax.axis_index("col"), lax.axis_index("rep")
    swap = [(p, 1 - p) for p in range(reps)]
    back = [(c, (c - 1) % cols) for c in range(cols)]
    flat = pair_rep.reshape(-1, chans)

    sends = rows // 2
    kept = flat.shape[0] // rows * (rows - 1)
    piece = kept // sends
    even = [0, 8, 6, -6, 4, -4, 2, -2]
    odd = [1, 7, -7, 5, -5, 3, -3, -1]
    got = []
    for s in range(sends):
        pairs = [(c * cols + c, (c + even[s]) % rows * cols + c) for c in range(cols)]
        pairs += [(c * cols + (c + 1) % cols, (c + odd[s]) % rows * cols + c) for c in range(cols)]
        message = jnp.concatenate([flat[s * piece : (s + 1) * piece], flat[kept:]])
        got.append(lax.ppermute(message, ("row", "col"), pairs))
    x_next = lax.ppermute(flat, "col", back)
    x_next, got = lax.optimization_barrier((x_next, got))
    order = jnp.array([o % rows for pair in zip(even, odd) for o in pair], jnp.int32)
    order = (order + col) % rows

    wrapped = jnp.concatenate([token_mask, token_mask[:tile]])
    mask_k = lax.dynamic_slice_in_dim(wrapped, col * tile, 2 * tile, 0).astype(F32).reshape(1, -1)
    mask_i = lax.dynamic_slice_in_dim(token_mask, row * tile + rep * half, half, 0)
    mask_j = lax.dynamic_slice_in_dim(token_mask, col * tile + rep * half, half, 0)

    left = left_call(mask_i, pair_rep, x_next.reshape(half, tile, chans), mask_k, w_a, w_a_gate)
    other = lax.ppermute(left, "rep", swap)

    chunk, rest = chunk_call(got, piece)
    rest_other = lax.ppermute(rest, "row", [(r, r ^ 1) for r in range(rows)])
    gathered = lax.all_gather(chunk, "row", axis=0, tiled=False)
    first = (row - col) % 2 == 0
    rests = (jnp.where(first, rest, rest_other), jnp.where(first, rest_other, rest))

    theirs, right = right_call(order, mask_j, gathered, *rests, mask_k, w_b, w_b_gate, other, w_out)
    received = lax.ppermute(theirs, "rep", swap)
    ours, gate = own_call(pair_rep, w_gate, left, right, w_out)
    received = received.astype(F32)
    low = rep == 0
    projected = jnp.concatenate([jnp.where(low, ours, received), jnp.where(low, received, ours)], axis=1)
    return (gate * projected).astype(BF16)


def solution(mesh):
    placed = (P(("row", "rep"), "col", None), P(), P(), P(), P(), P(), P(), P())
    return jax.shard_map(
        per_device,
        mesh=mesh,
        in_specs=placed,
        out_specs=P(("row", "rep"), "col", None),
        check_vma=False,
    )
```

```python
import functools

import jax
import jax.numpy as jnp
from jax import lax
from jax.experimental import pallas as pl
from jax.experimental.pallas import tpu as pltpu
from jax.sharding import PartitionSpec as P

EPS = 1e-5
VMEM = pl.BlockSpec(memory_space=pltpu.VMEM)
SMEM = pl.BlockSpec(memory_space=pltpu.SMEM)
F32 = jnp.float32
BF16 = jnp.bfloat16
GROUP = 16
LIMIT = 20 << 20


def dot(a, b, dims):
    return lax.dot_general(a, b, (dims, ((), ())), preferred_element_type=F32)


def normalise(block):
    chans = block.shape[1]
    ones = jnp.ones((chans, chans), BF16)
    centred = block.astype(F32) - dot(block, ones, ((1,), (0,))) * (1.0 / chans)
    var = dot((centred * centred).astype(BF16), ones, ((1,), (0,))) * (1.0 / chans)
    return (centred * lax.rsqrt(var + EPS)).astype(BF16)


def halved_transpose(w):
    return (w[...].astype(F32).T * 0.5).astype(BF16)


def gated(weights, normed, masks):
    hid = weights.shape[0] // 2
    both = dot(weights, normed, ((1,), (1,)))
    width = masks[0].shape[1]
    parts = []
    for n, mask in enumerate(masks):
        at = slice(n * width, (n + 1) * width)
        value = both[:hid, at] * mask
        parts.append(value + value * jnp.tanh(both[hid:, at]))
    return jnp.concatenate(parts, axis=1).reshape(hid, len(masks), width).astype(BF16)


def left_kernel(flags, x, x_next, mask_k, w, w_gate, v, v_gate, out, wt_right):
    half = x.shape[0]
    weights = jnp.concatenate([halved_transpose(w), halved_transpose(w_gate)])
    wt_right[...] = jnp.concatenate([halved_transpose(v), halved_transpose(v_gate)])
    for q in range(0, half, GROUP):
        blocks = [part[i] for i in range(q, q + GROUP) for part in (x, x_next)]
        masks = [mask_k[...] * flags[i].astype(F32) for i in range(q, q + GROUP)]
        out[:, q : q + GROUP, :] = gated(weights, normalise(jnp.concatenate(blocks)), masks)


def left_call(flags, x, x_next, mask_k, *ws):
    half, tile, chans = x.shape
    hid = ws[0].shape[1]
    return pl.pallas_call(
        left_kernel,
        out_shape=(
            jax.ShapeDtypeStruct((hid, half, 2 * tile), BF16),
            jax.ShapeDtypeStruct((2 * hid, chans), BF16),
        ),
        in_specs=[SMEM] + [VMEM] * 7,
        out_specs=(VMEM, VMEM),
        compiler_params=pltpu.CompilerParams(vmem_limit_bytes=LIMIT),
        name="left",
        cost_estimate=pl.CostEstimate(flops=10 * half * tile * 2 * chans * hid, bytes_accessed=2 << 20, transcendentals=4 * half * tile * hid),
    )(flags, x, x_next, mask_k, *ws)


def chunk_kernel(piece, *refs):
    *got, out, rest = refs
    total = got[0][...]
    for g in got[1:]:
        total = total + g[...]
    normed = normalise(total)
    out[...] = normed[:piece]
    rest[...] = normed[piece:]


def chunk_call(got, piece):
    n, chans = got[0].shape
    return pl.pallas_call(
        functools.partial(chunk_kernel, piece),
        out_shape=(jax.ShapeDtypeStruct((piece, chans), BF16), jax.ShapeDtypeStruct((n - piece, chans), BF16)),
        in_specs=[VMEM] * len(got),
        out_specs=(VMEM, VMEM),
        compiler_params=pltpu.CompilerParams(vmem_limit_bytes=LIMIT),
        name="chunk",
        cost_estimate=pl.CostEstimate(flops=4 * n * chans * chans, bytes_accessed=1 << 20, transcendentals=n * chans),
    )(*got)


def tri_projected(left, right, w_out, held, store):
    hid, half, _ = left.shape
    for c in range(0, hid, GROUP):
        parts = [dot(left[c + u], right[c + u], ((1,), (1,))) for u in range(GROUP)]
        held[:, c : c + GROUP, :] = jnp.swapaxes(jnp.stack(parts), 0, 1)
    pack = 128 // half
    for i in range(0, half, pack):
        tri = jnp.concatenate([held[i + u] for u in range(pack)], axis=1)
        mean = jnp.sum(tri, axis=0, keepdims=True) * (1.0 / hid)
        var = jnp.sum(tri * tri, axis=0, keepdims=True) * (1.0 / hid) - mean * mean
        normed = ((tri - mean) * lax.rsqrt(var + EPS)).astype(BF16)
        projected = dot(normed, w_out[...], ((0,), (0,)))
        for u in range(pack):
            store(i + u, projected[u * half : (u + 1) * half])


def right_kernel(order, flags, gathered, rest, rest_other, mask_k, weights, left, w_out, out, right, tiles, held):
    shards, piece, chans = gathered.shape
    hid, half, width = left.shape
    tile = width // 2
    kept = shards // 2 * piece
    for s in range(shards // 2):
        for t in range(2):
            tiles[t, s * piece : (s + 1) * piece] = gathered[order[2 * s + t]]
    tiles[order[shards], kept:] = rest[...]
    tiles[1 - order[shards], kept:] = rest_other[...]
    for q in range(0, half, GROUP):
        blocks = [tiles[t, j * tile : (j + 1) * tile] for j in range(q, q + GROUP) for t in range(2)]
        masks = [mask_k[...] * flags[j].astype(F32) for j in range(q, q + GROUP)]
        right[:, q : q + GROUP, :] = gated(weights[...], jnp.concatenate(blocks), masks)

    def store(i, rows):
        out[i] = rows.astype(BF16)

    tri_projected(left, right, w_out, held, store)


def right_call(order, flags, gathered, rest, rest_other, mask_k, weights, left, w_out):
    hid, half, width = left.shape
    chans = gathered.shape[-1]
    return pl.pallas_call(
        right_kernel,
        out_shape=(jax.ShapeDtypeStruct((half, half, chans), BF16), jax.ShapeDtypeStruct((hid, half, width), BF16)),
        in_specs=[SMEM] * 2 + [VMEM] * 7,
        out_specs=(VMEM, VMEM),
        scratch_shapes=[pltpu.VMEM((2, half * width // 2, chans), BF16), pltpu.VMEM((half, hid, half), F32)],
        compiler_params=pltpu.CompilerParams(vmem_limit_bytes=LIMIT),
        name="right_tri",
        cost_estimate=pl.CostEstimate(flops=8 * half * width * chans * hid, bytes_accessed=4 << 20, transcendentals=half * width * hid),
    )(order, flags, gathered, rest, rest_other, mask_k, weights, left, w_out)


def own_kernel(x, w_gate, left, right, w_out, out, gate, held):
    half, tile, chans = x.shape

    def store(i, rows):
        out[i] = rows

    tri_projected(left, right, w_out, held, store)
    for q in range(0, half, GROUP):
        normed = normalise(x[q : q + GROUP].reshape(GROUP * tile, chans))
        gate[q : q + GROUP] = jax.nn.sigmoid(dot(normed, w_gate[...], ((1,), (0,)))).reshape(GROUP, tile, chans)


def own_call(x, w_gate, left, right, w_out):
    half, tile, chans = x.shape
    hid = left.shape[0]
    return pl.pallas_call(
        own_kernel,
        out_shape=(jax.ShapeDtypeStruct((half, half, chans), F32), jax.ShapeDtypeStruct((half, tile, chans), F32)),
        in_specs=[VMEM] * 5,
        out_specs=(VMEM, VMEM),
        scratch_shapes=[pltpu.VMEM((half, hid, half), F32)],
        compiler_params=pltpu.CompilerParams(vmem_limit_bytes=LIMIT),
        name="own_tri",
        cost_estimate=pl.CostEstimate(flops=8 * half * tile * chans * chans, bytes_accessed=4 << 20, transcendentals=2 * half * tile * chans),
    )(x, w_gate, left, right, w_out)


def messages_kernel(kept, piece, flat, *outs):
    for s, out in enumerate(outs):
        out[:piece] = flat[s * piece : (s + 1) * piece]
        out[piece:] = flat[kept:]


def messages_call(flat, kept, sends):
    rows, chans = flat.shape
    piece = kept // sends
    shape = jax.ShapeDtypeStruct((piece + rows - kept, chans), flat.dtype)
    return pl.pallas_call(
        functools.partial(messages_kernel, kept, piece),
        out_shape=(shape,) * sends,
        in_specs=[VMEM],
        out_specs=(VMEM,) * sends,
        compiler_params=pltpu.CompilerParams(vmem_limit_bytes=LIMIT),
        name="messages",
        cost_estimate=pl.CostEstimate(flops=0, bytes_accessed=2 << 20, transcendentals=0),
    )(flat)


def per_device(pair_rep, token_mask, w_a, w_a_gate, w_b, w_b_gate, w_gate, w_out):
    half, tile, chans = pair_rep.shape
    rows, cols, reps = lax.axis_size("row"), lax.axis_size("col"), lax.axis_size("rep")
    row, col, rep = lax.axis_index("row"), lax.axis_index("col"), lax.axis_index("rep")
    swap = [(p, 1 - p) for p in range(reps)]
    flat = pair_rep.reshape(-1, chans)

    sends = rows // 2
    kept = flat.shape[0] // rows * (rows - 1)
    piece = kept // sends
    even = [8, 6, -6, 4, -4, 2, -2, 0]
    odd = [7, -7, 5, -5, 3, -3, 1, -1]
    got = []
    for s, message in enumerate(messages_call(flat, kept, sends)):
        pairs = [(c * cols + c, (c + even[s]) % rows * cols + c) for c in range(cols)]
        pairs += [(c * cols + (c + 1) % cols, (c + odd[s]) % rows * cols + c) for c in range(cols)]
        got.append(lax.ppermute(message, ("row", "col"), pairs))
    x_next = lax.ppermute(flat, "col", [(c, (c - 1) % cols) for c in range(cols)])
    x_next, got = lax.optimization_barrier((x_next, got))
    order = jnp.array([o % rows for pair in zip(even, odd) for o in pair], jnp.int32)
    order = jnp.concatenate([(order + col) % rows, (row + col).reshape(1) % 2])

    wrapped = jnp.concatenate([token_mask, token_mask[:tile]])
    mask_k = lax.dynamic_slice_in_dim(wrapped, col * tile, 2 * tile, 0).astype(F32).reshape(1, -1)
    mask_i = lax.dynamic_slice_in_dim(token_mask, row * tile + rep * half, half, 0)
    mask_j = lax.dynamic_slice_in_dim(token_mask, col * tile + rep * half, half, 0)

    left, wt_right = left_call(mask_i, pair_rep, x_next.reshape(half, tile, chans), mask_k, w_a, w_a_gate, w_b, w_b_gate)
    other = lax.ppermute(left, "rep", swap)

    chunk, rest = chunk_call(got, piece)
    rest_other = lax.ppermute(rest, "row", [(r, r ^ 1) for r in range(rows)])
    gathered = lax.all_gather(chunk, "row", axis=0, tiled=False)

    theirs, right = right_call(order, mask_j, gathered, rest, rest_other, mask_k, wt_right, other, w_out)
    received = lax.ppermute(theirs, "rep", swap)
    ours, gate = own_call(pair_rep, w_gate, left, right, w_out)
    received = received.astype(F32)
    low = rep == 0
    projected = jnp.concatenate([jnp.where(low, ours, received), jnp.where(low, received, ours)], axis=1)
    return (gate * projected).astype(BF16)


def solution(mesh):
    placed = (P(("row", "rep"), "col", None), P(), P(), P(), P(), P(), P(), P())
    return jax.shard_map(
        per_device,
        mesh=mesh,
        in_specs=placed,
        out_specs=P(("row", "rep"), "col", None),
        check_vma=False,
    )
```

```python
import functools

import jax
import jax.numpy as jnp
from jax import lax
from jax.experimental import pallas as pl
from jax.experimental.pallas import tpu as pltpu
from jax.sharding import PartitionSpec as P

EPS = 1e-5
VMEM = pl.BlockSpec(memory_space=pltpu.VMEM)
SMEM = pl.BlockSpec(memory_space=pltpu.SMEM)
HBM = pl.BlockSpec(memory_space=pl.ANY)
F32 = jnp.float32
BF16 = jnp.bfloat16
GROUP = 16
LIMIT = 20 << 20


def dot(a, b, dims):
    return lax.dot_general(a, b, (dims, ((), ())), preferred_element_type=F32)


def normalise(block):
    chans = block.shape[1]
    ones = jnp.ones((chans, chans), BF16)
    centred = block.astype(F32) - dot(block, ones, ((1,), (0,))) * (1.0 / chans)
    var = dot((centred * centred).astype(BF16), ones, ((1,), (0,))) * (1.0 / chans)
    return (centred * lax.rsqrt(var + EPS)).astype(BF16)


def halved_transpose(w):
    return (w[...].astype(F32).T * 0.5).astype(BF16)


def gated(weights, normed, masks):
    hid = weights.shape[0] // 2
    both = dot(weights, normed, ((1,), (1,)))
    width = masks[0].shape[1]
    parts = []
    for n, mask in enumerate(masks):
        at = slice(n * width, (n + 1) * width)
        value = both[:hid, at] * mask
        parts.append(value + value * jnp.tanh(both[hid:, at]))
    return jnp.concatenate(parts, axis=1).reshape(hid, len(masks), width).astype(BF16)


def left_kernel(flags, x, x_next, mask_k, weights, out):
    half = x.shape[0]
    for q in range(0, half, GROUP):
        blocks = [part[i] for i in range(q, q + GROUP) for part in (x, x_next)]
        masks = [mask_k[...] * flags[i].astype(F32) for i in range(q, q + GROUP)]
        out[:, q : q + GROUP, :] = gated(weights[...], normalise(jnp.concatenate(blocks)), masks)


def left_call(flags, x, x_next, mask_k, weights):
    half, tile, chans = x.shape
    hid = weights.shape[0] // 2
    return pl.pallas_call(
        left_kernel,
        out_shape=jax.ShapeDtypeStruct((hid, half, 2 * tile), BF16),
        in_specs=[SMEM] + [VMEM] * 4,
        out_specs=VMEM,
        compiler_params=pltpu.CompilerParams(vmem_limit_bytes=LIMIT),
        name="left",
        cost_estimate=pl.CostEstimate(flops=10 * half * tile * 2 * chans * hid, bytes_accessed=2 << 20, transcendentals=4 * half * tile * hid),
    )(flags, x, x_next, mask_k, weights)


def chunk_kernel(piece, *refs):
    *got, passed, out, rest = refs
    total = got[0][...]
    for g in got[1:]:
        total = total + g[...]
    own = jnp.concatenate([total[:piece], total[2 * piece :]])
    normed = normalise(own + passed[...])
    out[...] = normed[:piece]
    rest[...] = normed[piece:]


def chunk_call(got, passed, piece):
    n, chans = passed.shape
    return pl.pallas_call(
        functools.partial(chunk_kernel, piece),
        out_shape=(jax.ShapeDtypeStruct((piece, chans), BF16), jax.ShapeDtypeStruct((n - piece, chans), BF16)),
        in_specs=[VMEM] * (len(got) + 1),
        out_specs=(VMEM, VMEM),
        compiler_params=pltpu.CompilerParams(vmem_limit_bytes=LIMIT),
        name="chunk",
        cost_estimate=pl.CostEstimate(flops=4 * n * chans * chans, bytes_accessed=1 << 20, transcendentals=n * chans),
    )(*got, passed)


def tri_projected(left, right, w_out, held, store):
    hid, half, _ = left.shape
    for c in range(0, hid, GROUP):
        parts = [dot(left[c + u], right[c + u], ((1,), (1,))) for u in range(GROUP)]
        held[:, c : c + GROUP, :] = jnp.swapaxes(jnp.stack(parts), 0, 1)
    pack = 128 // half
    for i in range(0, half, pack):
        tri = jnp.concatenate([held[i + u] for u in range(pack)], axis=1)
        mean = jnp.sum(tri, axis=0, keepdims=True) * (1.0 / hid)
        var = jnp.sum(tri * tri, axis=0, keepdims=True) * (1.0 / hid) - mean * mean
        normed = ((tri - mean) * lax.rsqrt(var + EPS)).astype(BF16)
        projected = dot(normed, w_out[...], ((0,), (0,)))
        for u in range(pack):
            store(i + u, projected[u * half : (u + 1) * half])


def right_kernel(offsets, place, flags, gathered, rest, rest_other, mask_k, weights, left, w_out, out, right_out, tiles, right, held, sem):
    shards, piece, chans = gathered.shape
    hid, half, width = left.shape
    tile = width // 2
    kept = shards // 2 * piece
    for t in range(2):
        for s, offset in enumerate(offsets[t]):
            shard = lax.rem(place[0] + offset % shards, shards)
            tiles[t, s * piece : (s + 1) * piece] = gathered[shard]
    tiles[place[1], kept:] = rest[...]
    tiles[1 - place[1], kept:] = rest_other[...]
    for q in range(0, half, GROUP):
        blocks = [tiles[t, j * tile : (j + 1) * tile] for j in range(q, q + GROUP) for t in range(2)]
        masks = [mask_k[...] * flags[j].astype(F32) for j in range(q, q + GROUP)]
        right[:, q : q + GROUP, :] = gated(weights[...], jnp.concatenate(blocks), masks)
    copy = pltpu.make_async_copy(right, right_out, sem)
    copy.start()

    def store(i, rows):
        out[i] = rows.astype(BF16)

    tri_projected(left, right, w_out, held, store)
    copy.wait()


def right_call(offsets, place, flags, gathered, rest, rest_other, mask_k, weights, left, w_out):
    hid, half, width = left.shape
    chans = gathered.shape[-1]
    return pl.pallas_call(
        functools.partial(right_kernel, offsets),
        out_shape=(jax.ShapeDtypeStruct((half, half, chans), BF16), jax.ShapeDtypeStruct((hid, half, width), BF16)),
        in_specs=[SMEM] * 2 + [VMEM] * 7,
        out_specs=(VMEM, pl.BlockSpec(memory_space=pltpu.HBM)),
        scratch_shapes=[
            pltpu.VMEM((2, half * width // 2, chans), BF16),
            pltpu.VMEM((hid, half, width), BF16),
            pltpu.VMEM((half, hid, half), F32),
            pltpu.SemaphoreType.DMA,
        ],
        compiler_params=pltpu.CompilerParams(vmem_limit_bytes=LIMIT),
        name="right_tri",
        cost_estimate=pl.CostEstimate(flops=8 * half * width * chans * hid, bytes_accessed=4 << 20, transcendentals=half * width * hid),
    )(place, flags, gathered, rest, rest_other, mask_k, weights, left, w_out)


def own_kernel(x, w_gate, left, right, w_out, out, gate, held):
    half, tile, chans = x.shape

    def store(i, rows):
        out[i] = rows

    tri_projected(left, right, w_out, held, store)
    for q in range(0, half, GROUP):
        normed = normalise(x[q : q + GROUP].reshape(GROUP * tile, chans))
        gate[q : q + GROUP] = jax.nn.sigmoid(dot(normed, w_gate[...], ((1,), (0,)))).reshape(GROUP, tile, chans)


def own_call(x, w_gate, left, right, w_out):
    half, tile, chans = x.shape
    hid = left.shape[0]
    return pl.pallas_call(
        own_kernel,
        out_shape=(jax.ShapeDtypeStruct((half, half, chans), F32), jax.ShapeDtypeStruct((half, tile, chans), F32)),
        in_specs=[VMEM] * 5,
        out_specs=(VMEM, VMEM),
        scratch_shapes=[pltpu.VMEM((half, hid, half), F32)],
        compiler_params=pltpu.CompilerParams(vmem_limit_bytes=LIMIT),
        name="own_tri",
        cost_estimate=pl.CostEstimate(flops=8 * half * tile * chans * chans, bytes_accessed=4 << 20, transcendentals=2 * half * tile * chans),
    )(x, w_gate, left, right, w_out)


def first_kernel(sends, kept, *refs):
    flat, *ws = refs[:7]
    outs, (wt_left, wt_right, w_gate, w_out), held = refs[7 : 7 + sends], refs[7 + sends : 11 + sends], refs[11 + sends]
    sems = refs[-1]
    size = kept // sends
    copies = []
    for i, w in enumerate(ws):
        dst = (held.at[0], held.at[1], held.at[2], held.at[3], w_gate, w_out)[i]
        copies.append(pltpu.make_async_copy(w, dst, sems.at[i]))
    for s, out in enumerate(outs):
        copies.append(pltpu.make_async_copy(flat.at[s * size : (s + 1) * size], out.at[:size], sems.at[6 + 2 * s]))
        copies.append(pltpu.make_async_copy(flat.at[kept:], out.at[size:], sems.at[7 + 2 * s]))
    for copy in copies:
        copy.start()
    for copy in copies[:6]:
        copy.wait()
    hid = held.shape[1]
    for i, wt in enumerate((wt_left, wt_right)):
        wt[:hid] = halved_transpose(held.at[2 * i])
        wt[hid:] = halved_transpose(held.at[2 * i + 1])
    for copy in copies[6:]:
        copy.wait()


def first_call(flat, sends, kept, *ws):
    rows, chans = flat.shape
    hid = ws[0].shape[1]
    message = jax.ShapeDtypeStruct((kept // sends + rows - kept, chans), flat.dtype)
    weights = jax.ShapeDtypeStruct((2 * hid, chans), BF16)
    square = jax.ShapeDtypeStruct((chans, hid), BF16)
    return pl.pallas_call(
        functools.partial(first_kernel, sends, kept),
        out_shape=(message,) * sends + (weights, weights, square, square),
        in_specs=[HBM] * 7,
        out_specs=(VMEM,) * (sends + 4),
        scratch_shapes=[pltpu.VMEM((4, chans, hid), BF16), pltpu.SemaphoreType.DMA((6 + 2 * sends,))],
        compiler_params=pltpu.CompilerParams(vmem_limit_bytes=LIMIT),
        name="first",
        cost_estimate=pl.CostEstimate(flops=0, bytes_accessed=2 << 20, transcendentals=0),
    )(flat, *ws)


def per_device(pair_rep, token_mask, w_a, w_a_gate, w_b, w_b_gate, w_gate, w_out):
    half, tile, chans = pair_rep.shape
    rows, cols, reps = lax.axis_size("row"), lax.axis_size("col"), lax.axis_size("rep")
    row, col, rep = lax.axis_index("row"), lax.axis_index("col"), lax.axis_index("rep")
    swap = [(p, 1 - p) for p in range(reps)]
    flat = pair_rep.reshape(-1, chans)

    kept = flat.shape[0] // rows * (rows - 1)
    piece = kept // 8
    near = ((4, -2, 2, 0), (-3, 3, 1, -1))
    far = ((8, -6, 6, -4), (-7, 7, 5, -5))
    *messages, wt_left, wt_right, w_gate, w_out = first_call(flat, 4, kept, w_a, w_a_gate, w_b, w_b_gate, w_gate, w_out)
    got = []
    for s, message in enumerate(messages):
        pairs = [(c * cols + c, (c + near[0][s]) % rows * cols + c) for c in range(cols)]
        pairs += [(c * cols + (c + 1) % cols, (c + near[1][s]) % rows * cols + c) for c in range(cols)]
        got.append(lax.ppermute(message, ("row", "col"), pairs))
    x_next = lax.ppermute(flat, "col", [(c, (c - 1) % cols) for c in range(cols)])
    onward = got[0][piece:] + got[1][piece:] + got[2][piece:] + got[3][piece:]
    pairs = [
        ((c + n) % rows * cols + c, (c + f) % rows * cols + c)
        for c in range(cols)
        for t in range(2)
        for n, f in zip(near[t], far[t])
    ]
    passed = lax.ppermute(onward, ("row", "col"), pairs)
    offsets = tuple(tuple(o for pair in zip(near[t], far[t]) for o in pair) for t in range(2))
    place = jnp.stack([col, (row + col) % 2]).astype(jnp.int32)

    wrapped = jnp.concatenate([token_mask, token_mask[:tile]])
    mask_k = lax.dynamic_slice_in_dim(wrapped, col * tile, 2 * tile, 0).astype(F32).reshape(1, -1)
    mask_i = lax.dynamic_slice_in_dim(token_mask, row * tile + rep * half, half, 0)
    mask_j = lax.dynamic_slice_in_dim(token_mask, col * tile + rep * half, half, 0)

    x_next, passed = lax.optimization_barrier((x_next, passed))
    left = left_call(mask_i, pair_rep, x_next.reshape(half, tile, chans), mask_k, wt_left)
    other = lax.ppermute(left, "rep", swap)

    chunk, rest = chunk_call(got, passed, piece)
    rest_other = lax.ppermute(rest, "row", [(r, r ^ 1) for r in range(rows)])
    gathered = lax.all_gather(chunk, "row", axis=0, tiled=False)

    theirs, right = right_call(offsets, place, mask_j, gathered, rest, rest_other, mask_k, wt_right, other, w_out)
    received = lax.ppermute(theirs, "rep", swap)
    ours, gate = own_call(pair_rep, w_gate, left, right, w_out)
    received = received.astype(F32)
    low = rep == 0
    projected = jnp.concatenate([jnp.where(low, ours, received), jnp.where(low, received, ours)], axis=1)
    return (gate * projected).astype(BF16)


def solution(mesh):
    placed = (P(("row", "rep"), "col", None), P(), P(), P(), P(), P(), P(), P())
    return jax.shard_map(
        per_device,
        mesh=mesh,
        in_specs=placed,
        out_specs=P(("row", "rep"), "col", None),
        check_vma=False,
    )
```

```python
import functools

import jax
import jax.numpy as jnp
from jax import lax
from jax.experimental import pallas as pl
from jax.experimental.pallas import tpu as pltpu
from jax.sharding import PartitionSpec as P

EPS = 1e-5
VMEM = pl.BlockSpec(memory_space=pltpu.VMEM)
SMEM = pl.BlockSpec(memory_space=pltpu.SMEM)
HBM = pl.BlockSpec(memory_space=pl.ANY)
F32 = jnp.float32
BF16 = jnp.bfloat16
GROUP = 16
LIMIT = 20 << 20


def dot(a, b, dims):
    return lax.dot_general(a, b, (dims, ((), ())), preferred_element_type=F32)


def normalise(block):
    chans = block.shape[1]
    ones = jnp.ones((chans, chans), BF16)
    centred = block.astype(F32) - dot(block, ones, ((1,), (0,))) * (1.0 / chans)
    var = dot((centred * centred).astype(BF16), ones, ((1,), (0,))) * (1.0 / chans)
    return (centred * lax.rsqrt(var + EPS)).astype(BF16)


def halved_transpose(w):
    return (w[...].astype(F32).T * 0.5).astype(BF16)


def gated(weights, normed, masks):
    hid = weights.shape[0] // 2
    both = dot(weights, normed, ((1,), (1,)))
    width = masks[0].shape[1]
    parts = []
    for n, mask in enumerate(masks):
        at = slice(n * width, (n + 1) * width)
        value = both[:hid, at] * mask
        parts.append(value + value * jnp.tanh(both[hid:, at]))
    return jnp.concatenate(parts, axis=1).reshape(hid, len(masks), width).astype(BF16)


def left_kernel(flags, x, x_next, mask_k, weights, out):
    half = x.shape[0]
    for q in range(0, half, GROUP):
        blocks = [part[i] for i in range(q, q + GROUP) for part in (x, x_next)]
        masks = [mask_k[...] * flags[i].astype(F32) for i in range(q, q + GROUP)]
        out[:, q : q + GROUP, :] = gated(weights[...], normalise(jnp.concatenate(blocks)), masks)


def left_call(flags, x, x_next, mask_k, weights):
    half, tile, chans = x.shape
    hid = weights.shape[0] // 2
    return pl.pallas_call(
        left_kernel,
        out_shape=jax.ShapeDtypeStruct((hid, half, 2 * tile), BF16),
        in_specs=[SMEM] + [VMEM] * 4,
        out_specs=VMEM,
        compiler_params=pltpu.CompilerParams(vmem_limit_bytes=LIMIT),
        name="left",
        cost_estimate=pl.CostEstimate(flops=10 * half * tile * 2 * chans * hid, bytes_accessed=2 << 20, transcendentals=4 * half * tile * hid),
    )(flags, x, x_next, mask_k, weights)


def chunk_kernel(piece, *refs):
    *got, passed, out, rest = refs
    total = got[0][...]
    for g in got[1:]:
        total = total + g[...]
    own = jnp.concatenate([total[:piece], total[2 * piece :]])
    normed = normalise(own + passed[...])
    out[...] = normed[:piece]
    rest[...] = normed[piece:]


def chunk_call(got, passed, piece):
    n, chans = passed.shape
    return pl.pallas_call(
        functools.partial(chunk_kernel, piece),
        out_shape=(jax.ShapeDtypeStruct((piece, chans), BF16), jax.ShapeDtypeStruct((n - piece, chans), BF16)),
        in_specs=[VMEM] * (len(got) + 1),
        out_specs=(VMEM, VMEM),
        compiler_params=pltpu.CompilerParams(vmem_limit_bytes=LIMIT),
        name="chunk",
        cost_estimate=pl.CostEstimate(flops=4 * n * chans * chans, bytes_accessed=1 << 20, transcendentals=n * chans),
    )(*got, passed)


def tri_projected(left, right, w_out, held, store):
    hid, half, _ = left.shape
    for c in range(0, hid, GROUP):
        parts = [dot(left[c + u], right[c + u], ((1,), (1,))) for u in range(GROUP)]
        held[:, c : c + GROUP, :] = jnp.swapaxes(jnp.stack(parts), 0, 1)
    pack = 128 // half
    for i in range(0, half, pack):
        tri = jnp.concatenate([held[i + u] for u in range(pack)], axis=1)
        mean = jnp.sum(tri, axis=0, keepdims=True) * (1.0 / hid)
        var = jnp.sum(tri * tri, axis=0, keepdims=True) * (1.0 / hid) - mean * mean
        normed = ((tri - mean) * lax.rsqrt(var + EPS)).astype(BF16)
        projected = dot(normed, w_out[...], ((0,), (0,)))
        for u in range(pack):
            store(i + u, projected[u * half : (u + 1) * half])


def right_kernel(offsets, place, flags, gathered, rest, rest_other, mask_k, weights, left, w_out, out, right_out, tiles, right, held, sem):
    shards, piece, chans = gathered.shape
    hid, half, width = left.shape
    tile = width // 2
    kept = shards // 2 * piece
    for t in range(2):
        for s, offset in enumerate(offsets[t]):
            shard = lax.rem(place[0] + offset % shards, shards)
            tiles[t, s * piece : (s + 1) * piece] = gathered[shard]
    tiles[place[1], kept:] = rest[...]
    tiles[1 - place[1], kept:] = rest_other[...]
    for q in range(0, half, GROUP):
        blocks = [tiles[t, j * tile : (j + 1) * tile] for j in range(q, q + GROUP) for t in range(2)]
        masks = [mask_k[...] * flags[j].astype(F32) for j in range(q, q + GROUP)]
        right[:, q : q + GROUP, :] = gated(weights[...], jnp.concatenate(blocks), masks)
    copy = pltpu.make_async_copy(right, right_out, sem)
    copy.start()

    def store(i, rows):
        out[i] = rows.astype(BF16)

    tri_projected(left, right, w_out, held, store)
    copy.wait()


def right_call(offsets, place, flags, gathered, rest, rest_other, mask_k, weights, left, w_out):
    hid, half, width = left.shape
    chans = gathered.shape[-1]
    return pl.pallas_call(
        functools.partial(right_kernel, offsets),
        out_shape=(jax.ShapeDtypeStruct((half, half, chans), BF16), pltpu.HBM((hid, half, width), BF16)),
        in_specs=[SMEM] * 2 + [VMEM] * 7,
        out_specs=(VMEM, pl.BlockSpec(memory_space=pltpu.HBM)),
        scratch_shapes=[
            pltpu.VMEM((2, half * width // 2, chans), BF16),
            pltpu.VMEM((hid, half, width), BF16),
            pltpu.VMEM((half, hid, half), F32),
            pltpu.SemaphoreType.DMA,
        ],
        compiler_params=pltpu.CompilerParams(vmem_limit_bytes=LIMIT),
        name="right_tri",
        cost_estimate=pl.CostEstimate(flops=8 * half * width * chans * hid, bytes_accessed=4 << 20, transcendentals=half * width * hid),
    )(place, flags, gathered, rest, rest_other, mask_k, weights, left, w_out)


def own_kernel(x, w_gate, left, right, w_out, out, gate, held):
    half, tile, chans = x.shape

    def store(i, rows):
        out[i] = rows

    tri_projected(left, right, w_out, held, store)
    for q in range(0, half, GROUP):
        normed = normalise(x[q : q + GROUP].reshape(GROUP * tile, chans))
        gate[q : q + GROUP] = jax.nn.sigmoid(dot(normed, w_gate[...], ((1,), (0,)))).reshape(GROUP, tile, chans)


def own_call(x, w_gate, left, right, w_out):
    half, tile, chans = x.shape
    hid = left.shape[0]
    return pl.pallas_call(
        own_kernel,
        out_shape=(jax.ShapeDtypeStruct((half, half, chans), F32), jax.ShapeDtypeStruct((half, tile, chans), F32)),
        in_specs=[VMEM] * 5,
        out_specs=(VMEM, VMEM),
        scratch_shapes=[pltpu.VMEM((half, hid, half), F32)],
        compiler_params=pltpu.CompilerParams(vmem_limit_bytes=LIMIT),
        name="own_tri",
        cost_estimate=pl.CostEstimate(flops=8 * half * tile * chans * chans, bytes_accessed=4 << 20, transcendentals=2 * half * tile * chans),
    )(x, w_gate, left, right, w_out)


def first_kernel(sends, kept, *refs):
    flat, *ws = refs[:7]
    outs, (wt_left, wt_right, w_gate, w_out), held = refs[7 : 7 + sends], refs[7 + sends : 11 + sends], refs[11 + sends]
    sems = refs[-1]
    size = kept // sends
    copies = []
    for i, w in enumerate(ws):
        dst = (held.at[0], held.at[1], held.at[2], held.at[3], w_gate, w_out)[i]
        copies.append(pltpu.make_async_copy(w, dst, sems.at[i]))
    for s, out in enumerate(outs):
        copies.append(pltpu.make_async_copy(flat.at[s * size : (s + 1) * size], out.at[:size], sems.at[6 + 2 * s]))
        copies.append(pltpu.make_async_copy(flat.at[kept:], out.at[size:], sems.at[7 + 2 * s]))
    for copy in copies:
        copy.start()
    for copy in copies[:6]:
        copy.wait()
    hid = held.shape[1]
    for i, wt in enumerate((wt_left, wt_right)):
        wt[:hid] = halved_transpose(held.at[2 * i])
        wt[hid:] = halved_transpose(held.at[2 * i + 1])
    for copy in copies[6:]:
        copy.wait()


def first_call(flat, sends, kept, *ws):
    rows, chans = flat.shape
    hid = ws[0].shape[1]
    message = jax.ShapeDtypeStruct((kept // sends + rows - kept, chans), flat.dtype)
    weights = jax.ShapeDtypeStruct((2 * hid, chans), BF16)
    square = jax.ShapeDtypeStruct((chans, hid), BF16)
    return pl.pallas_call(
        functools.partial(first_kernel, sends, kept),
        out_shape=(message,) * sends + (weights, weights, square, square),
        in_specs=[HBM] * 7,
        out_specs=(VMEM,) * (sends + 4),
        scratch_shapes=[pltpu.VMEM((4, chans, hid), BF16), pltpu.SemaphoreType.DMA((6 + 2 * sends,))],
        compiler_params=pltpu.CompilerParams(vmem_limit_bytes=LIMIT),
        name="first",
        cost_estimate=pl.CostEstimate(flops=0, bytes_accessed=2 << 20, transcendentals=0),
    )(*(pltpu.with_memory_space_constraint(a, pltpu.HBM) for a in (flat, *ws)))


def per_device(pair_rep, token_mask, w_a, w_a_gate, w_b, w_b_gate, w_gate, w_out):
    half, tile, chans = pair_rep.shape
    rows, cols, reps = lax.axis_size("row"), lax.axis_size("col"), lax.axis_size("rep")
    row, col, rep = lax.axis_index("row"), lax.axis_index("col"), lax.axis_index("rep")
    swap = [(p, 1 - p) for p in range(reps)]
    flat = pair_rep.reshape(-1, chans)

    kept = flat.shape[0] // rows * (rows - 1)
    piece = kept // 8
    near = ((4, -2, 2, 0), (-3, 3, 1, -1))
    far = ((8, -6, 6, -4), (-7, 7, 5, -5))
    *messages, wt_left, wt_right, w_gate, w_out = first_call(flat, 4, kept, w_a, w_a_gate, w_b, w_b_gate, w_gate, w_out)
    got = []
    for s, message in enumerate(messages):
        pairs = [(c * cols + c, (c + near[0][s]) % rows * cols + c) for c in range(cols)]
        pairs += [(c * cols + (c + 1) % cols, (c + near[1][s]) % rows * cols + c) for c in range(cols)]
        got.append(lax.ppermute(message, ("row", "col"), pairs))
    x_next = lax.ppermute(flat, "col", [(c, (c - 1) % cols) for c in range(cols)])
    onward = got[0][piece:] + got[1][piece:] + got[2][piece:] + got[3][piece:]
    pairs = [
        ((c + n) % rows * cols + c, (c + f) % rows * cols + c)
        for c in range(cols)
        for t in range(2)
        for n, f in zip(near[t], far[t])
    ]
    passed = lax.ppermute(onward, ("row", "col"), pairs)
    offsets = tuple(tuple(o for pair in zip(near[t], far[t]) for o in pair) for t in range(2))
    place = jnp.stack([col, (row + col) % 2]).astype(jnp.int32)

    wrapped = jnp.concatenate([token_mask, token_mask[:tile]])
    mask_k = lax.dynamic_slice_in_dim(wrapped, col * tile, 2 * tile, 0).astype(F32).reshape(1, -1)
    mask_i = lax.dynamic_slice_in_dim(token_mask, row * tile + rep * half, half, 0)
    mask_j = lax.dynamic_slice_in_dim(token_mask, col * tile + rep * half, half, 0)

    x_next, passed = lax.optimization_barrier((x_next, passed))
    left = left_call(mask_i, pair_rep, x_next.reshape(half, tile, chans), mask_k, wt_left)
    other = lax.ppermute(left, "rep", swap)

    chunk, rest = chunk_call(got, passed, piece)
    rest_other = lax.ppermute(rest, "row", [(r, r ^ 1) for r in range(rows)])
    gathered = lax.all_gather(chunk, "row", axis=0, tiled=False)

    theirs, right = right_call(offsets, place, mask_j, gathered, rest, rest_other, mask_k, wt_right, other, w_out)
    received = lax.ppermute(theirs, "rep", swap)
    ours, gate = own_call(pair_rep, w_gate, left, right, w_out)
    received = received.astype(F32)
    low = rep == 0
    projected = jnp.concatenate([jnp.where(low, ours, received), jnp.where(low, received, ours)], axis=1)
    return (gate * projected).astype(BF16)


def solution(mesh):
    placed = (P(("row", "rep"), "col", None), P(), P(), P(), P(), P(), P(), P())
    return jax.shard_map(
        per_device,
        mesh=mesh,
        in_specs=placed,
        out_specs=P(("row", "rep"), "col", None),
        check_vma=False,
    )
```

```python
import functools

import jax
import jax.numpy as jnp
from jax import lax
from jax.experimental import pallas as pl
from jax.experimental.pallas import tpu as pltpu
from jax.sharding import PartitionSpec as P

EPS = 1e-5
VMEM = pl.BlockSpec(memory_space=pltpu.VMEM)
SMEM = pl.BlockSpec(memory_space=pltpu.SMEM)
HBM = pl.BlockSpec(memory_space=pl.ANY)
F32 = jnp.float32
BF16 = jnp.bfloat16
GROUP = 16
REST = 16
LIMIT = 20 << 20


def dot(a, b, dims):
    return lax.dot_general(a, b, (dims, ((), ())), preferred_element_type=F32)


def normalise(block):
    chans = block.shape[1]
    ones = jnp.ones((chans, chans), BF16)
    centred = block.astype(F32) - dot(block, ones, ((1,), (0,))) * (1.0 / chans)
    var = dot((centred * centred).astype(BF16), ones, ((1,), (0,))) * (1.0 / chans)
    return (centred * lax.rsqrt(var + EPS)).astype(BF16)


def halved_transpose(w):
    return (w[...].astype(F32).T * 0.5).astype(BF16)


def gated(weights, normed, masks):
    hid = weights.shape[0] // 2
    both = dot(weights, normed, ((1,), (1,)))
    width = masks[0].shape[1]
    parts = []
    for n, mask in enumerate(masks):
        at = slice(n * width, (n + 1) * width)
        value = both[:hid, at] * mask
        parts.append(value + value * jnp.tanh(both[hid:, at]))
    return jnp.concatenate(parts, axis=1).reshape(hid, len(masks), width).astype(BF16)


def left_kernel(flags, x, x_next, mask_k, weights, out):
    half = x.shape[0]
    for q in range(0, half, GROUP):
        blocks = [part[i] for i in range(q, q + GROUP) for part in (x, x_next)]
        masks = [mask_k[...] * flags[i].astype(F32) for i in range(q, q + GROUP)]
        out[:, q : q + GROUP, :] = gated(weights[...], normalise(jnp.concatenate(blocks)), masks)


def left_call(flags, x, x_next, mask_k, weights):
    half, tile, chans = x.shape
    hid = weights.shape[0] // 2
    return pl.pallas_call(
        left_kernel,
        out_shape=jax.ShapeDtypeStruct((hid, half, 2 * tile), BF16),
        in_specs=[SMEM] + [VMEM] * 4,
        out_specs=VMEM,
        compiler_params=pltpu.CompilerParams(vmem_limit_bytes=LIMIT),
        name="left",
        cost_estimate=pl.CostEstimate(flops=10 * half * tile * 2 * chans * hid, bytes_accessed=2 << 20, transcendentals=4 * half * tile * hid),
    )(flags, x, x_next, mask_k, weights)


def chunk_kernel(*refs):
    *got, passed, out, rest = refs
    total = got[0][...]
    for g in got[1:]:
        total = total + g[...]
    size = (total.shape[0] - REST) // 2
    own = jnp.concatenate([total[:size], total[2 * size :]])
    normed = normalise(own + passed[...])
    out[...] = normed[: size - 1]
    rest[...] = normed[size:]


def chunk_call(got, passed):
    n, chans = passed.shape
    return pl.pallas_call(
        chunk_kernel,
        out_shape=(jax.ShapeDtypeStruct((n - REST - 1, chans), BF16), jax.ShapeDtypeStruct((REST, chans), BF16)),
        in_specs=[VMEM] * (len(got) + 1),
        out_specs=(VMEM, VMEM),
        compiler_params=pltpu.CompilerParams(vmem_limit_bytes=LIMIT),
        name="chunk",
        cost_estimate=pl.CostEstimate(flops=4 * n * chans * chans, bytes_accessed=1 << 20, transcendentals=n * chans),
    )(*got, passed)


def tri_projected(left, right, w_out, held, store):
    hid, half, _ = left.shape
    for c in range(0, hid, GROUP):
        parts = [dot(left[c + u], right[c + u], ((1,), (1,))) for u in range(GROUP)]
        held[:, c : c + GROUP, :] = jnp.swapaxes(jnp.stack(parts), 0, 1)
    pack = 128 // half
    for i in range(0, half, pack):
        tri = jnp.concatenate([held[i + u] for u in range(pack)], axis=1)
        mean = jnp.sum(tri, axis=0, keepdims=True) * (1.0 / hid)
        var = jnp.sum(tri * tri, axis=0, keepdims=True) * (1.0 / hid) - mean * mean
        normed = ((tri - mean) * lax.rsqrt(var + EPS)).astype(BF16)
        projected = dot(normed, w_out[...], ((0,), (0,)))
        for u in range(pack):
            store(i + u, projected[u * half : (u + 1) * half])


def right_kernel(offsets, place, flags, gathered, rest, rest_other, mask_k, weights, left, w_out, out, right_out, tiles, rests, right, held, sem):
    shards, piece, _ = gathered.shape
    hid, half, width = left.shape
    tile = width // 2
    rests[place[1]] = rest[...].astype(F32)
    rests[1 - place[1]] = rest_other[...].astype(F32)
    whole = piece + 1 - REST
    for t in range(2):
        for s, offset in enumerate(offsets[t]):
            shard = lax.rem(place[0] + offset % shards, shards)
            at = s * (piece + 1)
            tiles[t, at : at + whole] = gathered[shard, :whole]
            last = jnp.concatenate([gathered[shard, whole:].astype(F32), rests[t, s : s + 1]])
            tiles[t, at + whole : at + whole + REST] = last.astype(BF16)
    for q in range(0, half, GROUP):
        blocks = [tiles[t, j * tile : (j + 1) * tile] for j in range(q, q + GROUP) for t in range(2)]
        masks = [mask_k[...] * flags[j].astype(F32) for j in range(q, q + GROUP)]
        right[:, q : q + GROUP, :] = gated(weights[...], jnp.concatenate(blocks), masks)
    copy = pltpu.make_async_copy(right, right_out, sem)
    copy.start()

    def store(i, rows):
        out[i] = rows.astype(BF16)

    tri_projected(left, right, w_out, held, store)
    copy.wait()


def right_call(offsets, place, flags, gathered, rest, rest_other, mask_k, weights, left, w_out):
    hid, half, width = left.shape
    chans = gathered.shape[-1]
    return pl.pallas_call(
        functools.partial(right_kernel, offsets),
        out_shape=(jax.ShapeDtypeStruct((half, half, chans), BF16), pltpu.HBM((hid, half, width), BF16)),
        in_specs=[SMEM] * 2 + [VMEM] * 7,
        out_specs=(VMEM, pl.BlockSpec(memory_space=pltpu.HBM)),
        scratch_shapes=[
            pltpu.VMEM((2, half * width // 2, chans), BF16),
            pltpu.VMEM((2, REST, chans), F32),
            pltpu.VMEM((hid, half, width), BF16),
            pltpu.VMEM((half, hid, half), F32),
            pltpu.SemaphoreType.DMA,
        ],
        compiler_params=pltpu.CompilerParams(vmem_limit_bytes=LIMIT),
        name="right_tri",
        cost_estimate=pl.CostEstimate(flops=8 * half * width * chans * hid, bytes_accessed=4 << 20, transcendentals=half * width * hid),
    )(place, flags, gathered, rest, rest_other, mask_k, weights, left, w_out)


def own_kernel(x, w_gate, left, right, w_out, out, gate, held):
    half, tile, chans = x.shape

    def store(i, rows):
        out[i] = rows

    tri_projected(left, right, w_out, held, store)
    for q in range(0, half, GROUP):
        normed = normalise(x[q : q + GROUP].reshape(GROUP * tile, chans))
        gate[q : q + GROUP] = jax.nn.sigmoid(dot(normed, w_gate[...], ((1,), (0,)))).reshape(GROUP, tile, chans)


def own_call(x, w_gate, left, right, w_out):
    half, tile, chans = x.shape
    hid = left.shape[0]
    return pl.pallas_call(
        own_kernel,
        out_shape=(jax.ShapeDtypeStruct((half, half, chans), F32), jax.ShapeDtypeStruct((half, tile, chans), F32)),
        in_specs=[VMEM] * 5,
        out_specs=(VMEM, VMEM),
        scratch_shapes=[pltpu.VMEM((half, hid, half), F32)],
        compiler_params=pltpu.CompilerParams(vmem_limit_bytes=LIMIT),
        name="own_tri",
        cost_estimate=pl.CostEstimate(flops=8 * half * tile * chans * chans, bytes_accessed=4 << 20, transcendentals=2 * half * tile * chans),
    )(x, w_gate, left, right, w_out)


def first_kernel(flat, *refs):
    *outs, tails, sems = refs
    chunks = 2 * len(outs)
    size = flat.shape[0] // chunks
    copies = []
    for s in range(chunks):
        end = (s + 1) * size
        copies.append(pltpu.make_async_copy(flat.at[end - REST : end], tails.at[s], sems.at[s]))
    for s, out in enumerate(outs):
        part = flat.at[2 * s * size : (2 * s + 2) * size]
        copies.append(pltpu.make_async_copy(part, out.at[: 2 * size], sems.at[chunks + s]))
    for copy in copies:
        copy.start()
    for copy in copies[:chunks]:
        copy.wait()
    rows = [tails[s].astype(F32)[REST - 1 :] for s in range(chunks)]
    rest = jnp.concatenate(rows + [jnp.zeros((REST - chunks, flat.shape[1]), F32)]).astype(BF16)
    for out in outs:
        out[2 * size :] = rest
    for copy in copies[chunks:]:
        copy.wait()


def first_call(flat, chunks):
    rows, chans = flat.shape
    sends = chunks // 2
    message = jax.ShapeDtypeStruct((rows // sends + REST, chans), flat.dtype)
    return pl.pallas_call(
        first_kernel,
        out_shape=(message,) * sends,
        in_specs=[HBM],
        out_specs=(VMEM,) * sends,
        scratch_shapes=[pltpu.VMEM((chunks, REST, chans), BF16), pltpu.SemaphoreType.DMA((chunks + sends,))],
        compiler_params=pltpu.CompilerParams(vmem_limit_bytes=LIMIT),
        name="first",
        cost_estimate=pl.CostEstimate(flops=0, bytes_accessed=2 << 20, transcendentals=0),
    )(pltpu.with_memory_space_constraint(flat, pltpu.HBM))


def weights_kernel(*refs):
    ws, (wt_left, wt_right, w_gate, w_out), held, sems = refs[:6], refs[6:10], refs[10], refs[11]
    copies = []
    for i, w in enumerate(ws):
        dst = (held.at[0], held.at[1], held.at[2], held.at[3], w_gate, w_out)[i]
        copies.append(pltpu.make_async_copy(w, dst, sems.at[i]))
    for copy in copies:
        copy.start()
    for copy in copies:
        copy.wait()
    hid = held.shape[2]
    for i, wt in enumerate((wt_left, wt_right)):
        wt[:hid] = halved_transpose(held.at[2 * i])
        wt[hid:] = halved_transpose(held.at[2 * i + 1])


def weights_call(*ws):
    chans, hid = ws[0].shape
    weights = jax.ShapeDtypeStruct((2 * hid, chans), BF16)
    square = jax.ShapeDtypeStruct((chans, hid), BF16)
    return pl.pallas_call(
        weights_kernel,
        out_shape=(weights, weights, square, square),
        in_specs=[HBM] * 6,
        out_specs=(VMEM,) * 4,
        scratch_shapes=[pltpu.VMEM((4, chans, hid), BF16), pltpu.SemaphoreType.DMA((6,))],
        compiler_params=pltpu.CompilerParams(vmem_limit_bytes=LIMIT),
        name="weights",
        cost_estimate=pl.CostEstimate(flops=0, bytes_accessed=1 << 20, transcendentals=0),
    )(*(pltpu.with_memory_space_constraint(w, pltpu.HBM) for w in ws))


def per_device(pair_rep, token_mask, w_a, w_a_gate, w_b, w_b_gate, w_gate, w_out):
    half, tile, chans = pair_rep.shape
    rows, cols, reps = lax.axis_size("row"), lax.axis_size("col"), lax.axis_size("rep")
    row, col, rep = lax.axis_index("row"), lax.axis_index("col"), lax.axis_index("rep")
    swap = [(p, 1 - p) for p in range(reps)]
    flat = pair_rep.reshape(-1, chans)

    near = ((0, 2, -2, 4), (1, -1, 3, -3))
    far = ((-4, 6, -6, 8), (5, -5, 7, -7))
    messages = first_call(flat, 8)
    chunk_rows = flat.shape[0] // 8
    got = []
    for s, message in enumerate(messages):
        pairs = [(c * cols + c, (c + near[0][s]) % rows * cols + c) for c in range(cols)]
        pairs += [(c * cols + (c + 1) % cols, (c + near[1][s]) % rows * cols + c) for c in range(cols)]
        got.append(lax.ppermute(message, ("row", "col"), pairs))
    wt_left, wt_right, w_gate, w_out = weights_call(w_a, w_a_gate, w_b, w_b_gate, w_gate, w_out)
    x_next = lax.ppermute(flat, "col", [(c, (c - 1) % cols) for c in range(cols)])
    onward = sum((g[chunk_rows:] for g in got[1:]), got[0][chunk_rows:])
    pairs = [
        ((c + n) % rows * cols + c, (c + f) % rows * cols + c)
        for c in range(cols)
        for t in range(2)
        for n, f in zip(near[t], far[t])
    ]
    passed = lax.ppermute(onward, ("row", "col"), pairs)
    offsets = tuple(tuple(o for pair in zip(near[t], far[t]) for o in pair) for t in range(2))
    place = jnp.stack([col, (row + col) % 2]).astype(jnp.int32)

    wrapped = jnp.concatenate([token_mask, token_mask[:tile]])
    mask_k = lax.dynamic_slice_in_dim(wrapped, col * tile, 2 * tile, 0).astype(F32).reshape(1, -1)
    mask_i = lax.dynamic_slice_in_dim(token_mask, row * tile + rep * half, half, 0)
    mask_j = lax.dynamic_slice_in_dim(token_mask, col * tile + rep * half, half, 0)

    left = left_call(mask_i, pair_rep, x_next.reshape(half, tile, chans), mask_k, wt_left)
    left, passed = lax.optimization_barrier((left, passed))
    other = lax.ppermute(left, "rep", swap)

    chunk, rest = chunk_call(got, passed)
    rest_other = lax.ppermute(rest, "row", [(r, r ^ 1) for r in range(rows)])
    gathered = lax.all_gather(chunk, "row", axis=0, tiled=False)

    theirs, right = right_call(offsets, place, mask_j, gathered, rest, rest_other, mask_k, wt_right, other, w_out)
    received = lax.ppermute(theirs, "rep", swap)
    ours, gate = own_call(pair_rep, w_gate, left, right, w_out)
    received = received.astype(F32)
    low = rep == 0
    projected = jnp.concatenate([jnp.where(low, ours, received), jnp.where(low, received, ours)], axis=1)
    return (gate * projected).astype(BF16)


def solution(mesh):
    placed = (P(("row", "rep"), "col", None), P(), P(), P(), P(), P(), P(), P())
    return jax.shard_map(
        per_device,
        mesh=mesh,
        in_specs=placed,
        out_specs=P(("row", "rep"), "col", None),
        check_vma=False,
    )
```

```python
import functools

import jax
import jax.numpy as jnp
from jax import lax
from jax.experimental import pallas as pl
from jax.experimental.pallas import tpu as pltpu
from jax.sharding import PartitionSpec as P

EPS = 1e-5
VMEM = pl.BlockSpec(memory_space=pltpu.VMEM)
SMEM = pl.BlockSpec(memory_space=pltpu.SMEM)
HBM = pl.BlockSpec(memory_space=pl.ANY)
F32 = jnp.float32
BF16 = jnp.bfloat16
GROUP = 16
REST = 16
LIMIT = 20 << 20


def dot(a, b, dims):
    return lax.dot_general(a, b, (dims, ((), ())), preferred_element_type=F32)


def normalise(block):
    chans = block.shape[1]
    ones = jnp.ones((chans, chans), BF16)
    centred = block.astype(F32) - dot(block, ones, ((1,), (0,))) * (1.0 / chans)
    var = dot((centred * centred).astype(BF16), ones, ((1,), (0,))) * (1.0 / chans)
    return (centred * lax.rsqrt(var + EPS)).astype(BF16)


def halved_transpose(w):
    return (w[...].astype(F32).T * 0.5).astype(BF16)


def gated(weights, normed, masks):
    hid = weights.shape[0] // 2
    both = dot(weights, normed, ((1,), (1,)))
    width = masks[0].shape[1]
    parts = []
    for n, mask in enumerate(masks):
        at = slice(n * width, (n + 1) * width)
        value = both[:hid, at] * mask
        parts.append(value + value * jnp.tanh(both[hid:, at]))
    return jnp.concatenate(parts, axis=1).reshape(hid, len(masks), width).astype(BF16)


def left_kernel(flags, x, x_next, mask_k, weights, out):
    half = x.shape[0]
    for q in range(0, half, GROUP):
        blocks = [part[i] for i in range(q, q + GROUP) for part in (x, x_next)]
        masks = [mask_k[...] * flags[i].astype(F32) for i in range(q, q + GROUP)]
        out[:, q : q + GROUP, :] = gated(weights[...], normalise(jnp.concatenate(blocks)), masks)


def left_call(flags, x, x_next, mask_k, weights):
    half, tile, chans = x.shape
    hid = weights.shape[0] // 2
    return pl.pallas_call(
        left_kernel,
        out_shape=jax.ShapeDtypeStruct((hid, half, 2 * tile), BF16),
        in_specs=[SMEM] + [VMEM] * 4,
        out_specs=VMEM,
        compiler_params=pltpu.CompilerParams(vmem_limit_bytes=LIMIT),
        name="left",
        cost_estimate=pl.CostEstimate(flops=10 * half * tile * 2 * chans * hid, bytes_accessed=2 << 20, transcendentals=4 * half * tile * hid),
    )(flags, x, x_next, mask_k, weights)


def chunk_kernel(*refs):
    *got, passed, out, rest = refs
    total = got[0][...]
    for g in got[1:]:
        total = total + g[...]
    size = (total.shape[0] - REST) // 2
    own = jnp.concatenate([total[:size], total[2 * size :]])
    normed = normalise(own + passed[...])
    out[...] = normed[: size - 1]
    rest[...] = normed[size:]


def chunk_call(got, passed):
    n, chans = passed.shape
    return pl.pallas_call(
        chunk_kernel,
        out_shape=(jax.ShapeDtypeStruct((n - REST - 1, chans), BF16), jax.ShapeDtypeStruct((REST, chans), BF16)),
        in_specs=[VMEM] * (len(got) + 1),
        out_specs=(VMEM, VMEM),
        compiler_params=pltpu.CompilerParams(vmem_limit_bytes=LIMIT),
        name="chunk",
        cost_estimate=pl.CostEstimate(flops=4 * n * chans * chans, bytes_accessed=1 << 20, transcendentals=n * chans),
    )(*got, passed)


def tri_projected(left, right, w_out, held, store):
    hid, half, _ = left.shape
    for c in range(0, hid, GROUP):
        parts = [dot(left[c + u], right[c + u], ((1,), (1,))) for u in range(GROUP)]
        held[:, c : c + GROUP, :] = jnp.swapaxes(jnp.stack(parts), 0, 1)
    pack = 128 // half
    for i in range(0, half, pack):
        tri = jnp.concatenate([held[i + u] for u in range(pack)], axis=1)
        mean = jnp.sum(tri, axis=0, keepdims=True) * (1.0 / hid)
        var = jnp.sum(tri * tri, axis=0, keepdims=True) * (1.0 / hid) - mean * mean
        normed = ((tri - mean) * lax.rsqrt(var + EPS)).astype(BF16)
        projected = dot(normed, w_out[...], ((0,), (0,)))
        for u in range(pack):
            store(i + u, projected[u * half : (u + 1) * half])


def right_kernel(offsets, place, flags, gathered, rest, rest_other, mask_k, weights, right, tiles, rests):
    shards, piece, _ = gathered.shape
    hid, half, width = right.shape
    tile = width // 2
    rests[place[1]] = rest[...].astype(F32)
    rests[1 - place[1]] = rest_other[...].astype(F32)
    whole = piece + 1 - REST
    for t in range(2):
        for s, offset in enumerate(offsets[t]):
            shard = lax.rem(place[0] + offset % shards, shards)
            at = s * (piece + 1)
            tiles[t, at : at + whole] = gathered[shard, :whole]
            last = jnp.concatenate([gathered[shard, whole:].astype(F32), rests[t, s : s + 1]])
            tiles[t, at + whole : at + whole + REST] = last.astype(BF16)
    for q in range(0, half, GROUP):
        blocks = [tiles[t, j * tile : (j + 1) * tile] for j in range(q, q + GROUP) for t in range(2)]
        masks = [mask_k[...] * flags[j].astype(F32) for j in range(q, q + GROUP)]
        right[:, q : q + GROUP, :] = gated(weights[...], jnp.concatenate(blocks), masks)


def right_call(offsets, place, flags, gathered, rest, rest_other, mask_k, weights):
    half, chans = flags.shape[0], gathered.shape[-1]
    hid, width = weights.shape[0] // 2, mask_k.shape[1]
    return pl.pallas_call(
        functools.partial(right_kernel, offsets),
        out_shape=jax.ShapeDtypeStruct((hid, half, width), BF16),
        in_specs=[SMEM] * 2 + [VMEM] * 5,
        out_specs=VMEM,
        scratch_shapes=[pltpu.VMEM((2, half * width // 2, chans), BF16), pltpu.VMEM((2, REST, chans), F32)],
        compiler_params=pltpu.CompilerParams(vmem_limit_bytes=LIMIT),
        name="right",
        cost_estimate=pl.CostEstimate(flops=5 * 10**9, bytes_accessed=4 << 20, transcendentals=half * width * hid),
    )(place, flags, gathered, rest, rest_other, mask_k, weights)


def theirs_kernel(left, right, w_out, out, held):
    def store(i, rows):
        out[i] = rows.astype(BF16)

    tri_projected(left, right, w_out, held, store)


def theirs_call(left, right, w_out):
    hid, half, _ = left.shape
    chans = w_out.shape[1]
    return pl.pallas_call(
        theirs_kernel,
        out_shape=jax.ShapeDtypeStruct((half, half, chans), BF16),
        in_specs=[VMEM] * 3,
        out_specs=VMEM,
        scratch_shapes=[pltpu.VMEM((half, hid, half), F32)],
        compiler_params=pltpu.CompilerParams(vmem_limit_bytes=LIMIT),
        name="theirs",
        cost_estimate=pl.CostEstimate(flops=8 * half * half * chans * hid, bytes_accessed=2 << 20, transcendentals=0),
    )(left, right, w_out)


def own_kernel(x, w_gate, left, right, w_out, out, gate, held):
    half, tile, chans = x.shape

    def store(i, rows):
        out[i] = rows

    tri_projected(left, right, w_out, held, store)
    for q in range(0, half, GROUP):
        normed = normalise(x[q : q + GROUP].reshape(GROUP * tile, chans))
        gate[q : q + GROUP] = jax.nn.sigmoid(dot(normed, w_gate[...], ((1,), (0,)))).reshape(GROUP, tile, chans)


def own_call(x, w_gate, left, right, w_out):
    half, tile, chans = x.shape
    hid = left.shape[0]
    return pl.pallas_call(
        own_kernel,
        out_shape=(jax.ShapeDtypeStruct((half, half, chans), F32), jax.ShapeDtypeStruct((half, tile, chans), F32)),
        in_specs=[VMEM] * 5,
        out_specs=(VMEM, VMEM),
        scratch_shapes=[pltpu.VMEM((half, hid, half), F32)],
        compiler_params=pltpu.CompilerParams(vmem_limit_bytes=LIMIT),
        name="own_tri",
        cost_estimate=pl.CostEstimate(flops=8 * half * tile * chans * chans, bytes_accessed=4 << 20, transcendentals=2 * half * tile * chans),
    )(x, w_gate, left, right, w_out)


def first_kernel(flat, *refs):
    *outs, tails, sems = refs
    chunks = 2 * len(outs)
    size = flat.shape[0] // chunks
    copies = []
    for s in range(chunks):
        end = (s + 1) * size
        copies.append(pltpu.make_async_copy(flat.at[end - REST : end], tails.at[s], sems.at[s]))
    for s, out in enumerate(outs):
        part = flat.at[2 * s * size : (2 * s + 2) * size]
        copies.append(pltpu.make_async_copy(part, out.at[: 2 * size], sems.at[chunks + s]))
    for copy in copies:
        copy.start()
    for copy in copies[:chunks]:
        copy.wait()
    rows = [tails[s].astype(F32)[REST - 1 :] for s in range(chunks)]
    rest = jnp.concatenate(rows + [jnp.zeros((REST - chunks, flat.shape[1]), F32)]).astype(BF16)
    for out in outs:
        out[2 * size :] = rest
    for copy in copies[chunks:]:
        copy.wait()


def first_call(flat, chunks):
    rows, chans = flat.shape
    sends = chunks // 2
    message = jax.ShapeDtypeStruct((rows // sends + REST, chans), flat.dtype)
    return pl.pallas_call(
        first_kernel,
        out_shape=(message,) * sends,
        in_specs=[HBM],
        out_specs=(VMEM,) * sends,
        scratch_shapes=[pltpu.VMEM((chunks, REST, chans), BF16), pltpu.SemaphoreType.DMA((chunks + sends,))],
        compiler_params=pltpu.CompilerParams(vmem_limit_bytes=LIMIT),
        name="first",
        cost_estimate=pl.CostEstimate(flops=0, bytes_accessed=2 << 20, transcendentals=0),
    )(pltpu.with_memory_space_constraint(flat, pltpu.HBM))


def weights_kernel(*refs):
    ws, (wt_left, wt_right, w_gate, w_out), held, sems = refs[:6], refs[6:10], refs[10], refs[11]
    copies = []
    for i, w in enumerate(ws):
        dst = (held.at[0], held.at[1], held.at[2], held.at[3], w_gate, w_out)[i]
        copies.append(pltpu.make_async_copy(w, dst, sems.at[i]))
    for copy in copies:
        copy.start()
    for copy in copies:
        copy.wait()
    hid = held.shape[2]
    for i, wt in enumerate((wt_left, wt_right)):
        wt[:hid] = halved_transpose(held.at[2 * i])
        wt[hid:] = halved_transpose(held.at[2 * i + 1])


def weights_call(*ws):
    chans, hid = ws[0].shape
    weights = jax.ShapeDtypeStruct((2 * hid, chans), BF16)
    square = jax.ShapeDtypeStruct((chans, hid), BF16)
    return pl.pallas_call(
        weights_kernel,
        out_shape=(weights, weights, square, square),
        in_specs=[HBM] * 6,
        out_specs=(VMEM,) * 4,
        scratch_shapes=[pltpu.VMEM((4, chans, hid), BF16), pltpu.SemaphoreType.DMA((6,))],
        compiler_params=pltpu.CompilerParams(vmem_limit_bytes=LIMIT),
        name="weights",
        cost_estimate=pl.CostEstimate(flops=10**10, bytes_accessed=1 << 20, transcendentals=0),
    )(*(pltpu.with_memory_space_constraint(w, pltpu.HBM) for w in ws))


def per_device(pair_rep, token_mask, w_a, w_a_gate, w_b, w_b_gate, w_gate, w_out):
    half, tile, chans = pair_rep.shape
    rows, cols, reps = lax.axis_size("row"), lax.axis_size("col"), lax.axis_size("rep")
    row, col, rep = lax.axis_index("row"), lax.axis_index("col"), lax.axis_index("rep")
    swap = [(p, 1 - p) for p in range(reps)]
    flat = pair_rep.reshape(-1, chans)

    near = ((0, 2, -2, 4), (1, -1, 3, -3))
    far = ((-4, 6, -6, 8), (5, -5, 7, -7))
    messages = first_call(flat, 8)
    chunk_rows = flat.shape[0] // 8
    got = []
    for s, message in enumerate(messages):
        pairs = [(c * cols + c, (c + near[0][s]) % rows * cols + c) for c in range(cols)]
        pairs += [(c * cols + (c + 1) % cols, (c + near[1][s]) % rows * cols + c) for c in range(cols)]
        got.append(lax.ppermute(message, ("row", "col"), pairs))
    wt_left, wt_right, w_gate, w_out = weights_call(w_a, w_a_gate, w_b, w_b_gate, w_gate, w_out)
    flat, messages = lax.optimization_barrier((flat, messages))
    x_next = lax.ppermute(flat, "col", [(c, (c - 1) % cols) for c in range(cols)])
    onward = sum((g[chunk_rows:] for g in got[1:]), got[0][chunk_rows:])
    pairs = [
        ((c + n) % rows * cols + c, (c + f) % rows * cols + c)
        for c in range(cols)
        for t in range(2)
        for n, f in zip(near[t], far[t])
    ]
    passed = lax.ppermute(onward, ("row", "col"), pairs)
    offsets = tuple(tuple(o for pair in zip(near[t], far[t]) for o in pair) for t in range(2))
    place = jnp.stack([col, (row + col) % 2]).astype(jnp.int32)

    wrapped = jnp.concatenate([token_mask, token_mask[:tile]])
    mask_k = lax.dynamic_slice_in_dim(wrapped, col * tile, 2 * tile, 0).astype(F32).reshape(1, -1)
    mask_i = lax.dynamic_slice_in_dim(token_mask, row * tile + rep * half, half, 0)
    mask_j = lax.dynamic_slice_in_dim(token_mask, col * tile + rep * half, half, 0)

    left = left_call(mask_i, pair_rep, x_next.reshape(half, tile, chans), mask_k, wt_left)
    other = lax.ppermute(left, "rep", swap)

    chunk, rest = chunk_call(got, passed)
    rest_other = lax.ppermute(rest, "row", [(r, r ^ 1) for r in range(rows)])
    gathered = lax.all_gather(chunk, "row", axis=0, tiled=False)

    right = right_call(offsets, place, mask_j, gathered, rest, rest_other, mask_k, wt_right)
    theirs = theirs_call(other, right, w_out)
    received = lax.ppermute(theirs, "rep", swap)
    ours, gate = own_call(pair_rep, w_gate, left, right, w_out)
    received = received.astype(F32)
    low = rep == 0
    projected = jnp.concatenate([jnp.where(low, ours, received), jnp.where(low, received, ours)], axis=1)
    return (gate * projected).astype(BF16)


def solution(mesh):
    placed = (P(("row", "rep"), "col", None), P(), P(), P(), P(), P(), P(), P())
    return jax.shard_map(
        per_device,
        mesh=mesh,
        in_specs=placed,
        out_specs=P(("row", "rep"), "col", None),
        check_vma=False,
    )
```

```python
import functools

import jax
import jax.numpy as jnp
from jax import lax
from jax.experimental import pallas as pl
from jax.experimental.pallas import tpu as pltpu
from jax.sharding import PartitionSpec as P

EPS = 1e-5
VMEM = pl.BlockSpec(memory_space=pltpu.VMEM)
SMEM = pl.BlockSpec(memory_space=pltpu.SMEM)
HBM = pl.BlockSpec(memory_space=pl.ANY)
F32 = jnp.float32
BF16 = jnp.bfloat16
GROUP = 16
REST = 16
LIMIT = 20 << 20


def dot(a, b, dims):
    return lax.dot_general(a, b, (dims, ((), ())), preferred_element_type=F32)


def normalise(block):
    chans = block.shape[1]
    ones = jnp.ones((chans, chans), BF16)
    centred = block.astype(F32) - dot(block, ones, ((1,), (0,))) * (1.0 / chans)
    var = dot((centred * centred).astype(BF16), ones, ((1,), (0,))) * (1.0 / chans)
    return (centred * lax.rsqrt(var + EPS)).astype(BF16)


def halved_transpose(w):
    return (w[...].astype(F32).T * 0.5).astype(BF16)


def gated(weights, normed, masks):
    hid = weights.shape[0] // 2
    both = dot(weights, normed, ((1,), (1,)))
    width = masks[0].shape[1]
    parts = []
    for n, mask in enumerate(masks):
        at = slice(n * width, (n + 1) * width)
        value = both[:hid, at] * mask
        parts.append(value + value * jnp.tanh(both[hid:, at]))
    return jnp.concatenate(parts, axis=1).reshape(hid, len(masks), width).astype(BF16)


def left_kernel(flags, x, x_next, mask_k, weights, out):
    half = x.shape[0]
    for q in range(0, half, GROUP):
        blocks = [part[i] for i in range(q, q + GROUP) for part in (x, x_next)]
        masks = [mask_k[...] * flags[i].astype(F32) for i in range(q, q + GROUP)]
        out[:, q : q + GROUP, :] = gated(weights[...], normalise(jnp.concatenate(blocks)), masks)


def left_call(flags, x, x_next, mask_k, weights):
    half, tile, chans = x.shape
    hid = weights.shape[0] // 2
    return pl.pallas_call(
        left_kernel,
        out_shape=jax.ShapeDtypeStruct((hid, half, 2 * tile), BF16),
        in_specs=[SMEM] + [VMEM] * 4,
        out_specs=VMEM,
        compiler_params=pltpu.CompilerParams(vmem_limit_bytes=LIMIT),
        name="left",
        cost_estimate=pl.CostEstimate(flops=10 * half * tile * 2 * chans * hid, bytes_accessed=2 << 20, transcendentals=4 * half * tile * hid),
    )(flags, x, x_next, mask_k, weights)


def chunk_kernel(*refs):
    *got, passed, out, rest = refs
    total = got[0][...]
    for g in got[1:]:
        total = total + g[...]
    size = (total.shape[0] - REST) // 2
    own = jnp.concatenate([total[:size], total[2 * size :]])
    normed = normalise(own + passed[...])
    out[...] = normed[: size - 1]
    rest[...] = normed[size:]


def chunk_call(got, passed):
    n, chans = passed.shape
    return pl.pallas_call(
        chunk_kernel,
        out_shape=(jax.ShapeDtypeStruct((n - REST - 1, chans), BF16), jax.ShapeDtypeStruct((REST, chans), BF16)),
        in_specs=[VMEM] * (len(got) + 1),
        out_specs=(VMEM, VMEM),
        compiler_params=pltpu.CompilerParams(vmem_limit_bytes=LIMIT),
        name="chunk",
        cost_estimate=pl.CostEstimate(flops=4 * n * chans * chans, bytes_accessed=1 << 20, transcendentals=n * chans),
    )(*got, passed)


def tri_projected(left, right, w_out, held, store):
    hid, half, _ = left.shape
    for c in range(0, hid, GROUP):
        parts = [dot(left[c + u], right[c + u], ((1,), (1,))) for u in range(GROUP)]
        held[:, c : c + GROUP, :] = jnp.swapaxes(jnp.stack(parts), 0, 1)
    pack = 128 // half
    for i in range(0, half, pack):
        tri = jnp.concatenate([held[i + u] for u in range(pack)], axis=1)
        mean = jnp.sum(tri, axis=0, keepdims=True) * (1.0 / hid)
        var = jnp.sum(tri * tri, axis=0, keepdims=True) * (1.0 / hid) - mean * mean
        normed = ((tri - mean) * lax.rsqrt(var + EPS)).astype(BF16)
        projected = dot(normed, w_out[...], ((0,), (0,)))
        for u in range(pack):
            store(i + u, projected[u * half : (u + 1) * half])


def right_kernel(offsets, place, flags, gathered, rest, rest_other, mask_k, weights, right, tiles, rests):
    shards, piece, _ = gathered.shape
    hid, half, width = right.shape
    tile = width // 2
    rests[place[1]] = rest[...].astype(F32)
    rests[1 - place[1]] = rest_other[...].astype(F32)
    whole = piece + 1 - REST
    for t in range(2):
        for s, offset in enumerate(offsets[t]):
            shard = lax.rem(place[0] + offset % shards, shards)
            at = s * (piece + 1)
            tiles[t, at : at + whole] = gathered[shard, :whole]
            last = jnp.concatenate([gathered[shard, whole:].astype(F32), rests[t, s : s + 1]])
            tiles[t, at + whole : at + whole + REST] = last.astype(BF16)
    for q in range(0, half, GROUP):
        blocks = [tiles[t, j * tile : (j + 1) * tile] for j in range(q, q + GROUP) for t in range(2)]
        masks = [mask_k[...] * flags[j].astype(F32) for j in range(q, q + GROUP)]
        right[:, q : q + GROUP, :] = gated(weights[...], jnp.concatenate(blocks), masks)


def right_call(offsets, place, flags, gathered, rest, rest_other, mask_k, weights):
    half, chans = flags.shape[0], gathered.shape[-1]
    hid, width = weights.shape[0] // 2, mask_k.shape[1]
    return pl.pallas_call(
        functools.partial(right_kernel, offsets),
        out_shape=jax.ShapeDtypeStruct((hid, half, width), BF16),
        in_specs=[SMEM] * 2 + [VMEM] * 5,
        out_specs=VMEM,
        scratch_shapes=[pltpu.VMEM((2, half * width // 2, chans), BF16), pltpu.VMEM((2, REST, chans), F32)],
        compiler_params=pltpu.CompilerParams(vmem_limit_bytes=LIMIT),
        name="right",
        cost_estimate=pl.CostEstimate(flops=5 * 10**9, bytes_accessed=4 << 20, transcendentals=half * width * hid),
    )(place, flags, gathered, rest, rest_other, mask_k, weights)


def theirs_kernel(left, right, w_out, out, held):
    def store(i, rows):
        out[i] = rows.astype(BF16)

    tri_projected(left, right, w_out, held, store)


def theirs_call(left, right, w_out):
    hid, half, _ = left.shape
    chans = w_out.shape[1]
    return pl.pallas_call(
        theirs_kernel,
        out_shape=jax.ShapeDtypeStruct((half, half, chans), BF16),
        in_specs=[VMEM] * 3,
        out_specs=VMEM,
        scratch_shapes=[pltpu.VMEM((half, hid, half), F32)],
        compiler_params=pltpu.CompilerParams(vmem_limit_bytes=LIMIT),
        name="theirs",
        cost_estimate=pl.CostEstimate(flops=8 * half * half * chans * hid, bytes_accessed=2 << 20, transcendentals=0),
    )(left, right, w_out)


def own_kernel(x, w_gate, left, right, w_out, out, gate, held):
    half, tile, chans = x.shape

    def store(i, rows):
        out[i] = rows

    tri_projected(left, right, w_out, held, store)
    for q in range(0, half, GROUP):
        normed = normalise(x[q : q + GROUP].reshape(GROUP * tile, chans))
        gate[q : q + GROUP] = jax.nn.sigmoid(dot(normed, w_gate[...], ((1,), (0,)))).reshape(GROUP, tile, chans)


def own_call(x, w_gate, left, right, w_out):
    half, tile, chans = x.shape
    hid = left.shape[0]
    return pl.pallas_call(
        own_kernel,
        out_shape=(jax.ShapeDtypeStruct((half, half, chans), F32), jax.ShapeDtypeStruct((half, tile, chans), F32)),
        in_specs=[VMEM] * 5,
        out_specs=(VMEM, VMEM),
        scratch_shapes=[pltpu.VMEM((half, hid, half), F32)],
        compiler_params=pltpu.CompilerParams(vmem_limit_bytes=LIMIT),
        name="own_tri",
        cost_estimate=pl.CostEstimate(flops=8 * half * tile * chans * chans, bytes_accessed=4 << 20, transcendentals=2 * half * tile * chans),
    )(x, w_gate, left, right, w_out)


def first_kernel(flat, *refs):
    *outs, tails, sems = refs
    chunks = 2 * len(outs)
    size = flat.shape[0] // chunks
    ahead = lax.axis_index("col") - lax.axis_index("row") + lax.axis_size("col")

    @pl.when(lax.rem(ahead, lax.axis_size("col")) < 2)
    def _():
        copies = []
        for s in range(chunks):
            end = (s + 1) * size
            copies.append(pltpu.make_async_copy(flat.at[end - REST : end], tails.at[s], sems.at[s]))
        for s, out in enumerate(outs):
            part = flat.at[2 * s * size : (2 * s + 2) * size]
            copies.append(pltpu.make_async_copy(part, out.at[: 2 * size], sems.at[chunks + s]))
        for copy in copies:
            copy.start()
        for copy in copies[:chunks]:
            copy.wait()
        rows = [tails[s].astype(F32)[REST - 1 :] for s in range(chunks)]
        rest = jnp.concatenate(rows + [jnp.zeros((REST - chunks, flat.shape[1]), F32)]).astype(BF16)
        for out in outs:
            out[2 * size :] = rest
        for copy in copies[chunks:]:
            copy.wait()


def first_call(flat, chunks):
    rows, chans = flat.shape
    sends = chunks // 2
    message = jax.ShapeDtypeStruct((rows // sends + REST, chans), flat.dtype)
    return pl.pallas_call(
        first_kernel,
        out_shape=(message,) * sends,
        in_specs=[HBM],
        out_specs=(VMEM,) * sends,
        scratch_shapes=[pltpu.VMEM((chunks, REST, chans), BF16), pltpu.SemaphoreType.DMA((chunks + sends,))],
        compiler_params=pltpu.CompilerParams(vmem_limit_bytes=LIMIT),
        name="first",
        cost_estimate=pl.CostEstimate(flops=0, bytes_accessed=2 << 20, transcendentals=0),
    )(pltpu.with_memory_space_constraint(flat, pltpu.HBM))


def weights_kernel(*refs):
    ws, (wt_left, wt_right, w_gate, w_out), held, sems = refs[:6], refs[6:10], refs[10], refs[11]
    copies = []
    for i, w in enumerate(ws):
        dst = (held.at[0], held.at[1], held.at[2], held.at[3], w_gate, w_out)[i]
        copies.append(pltpu.make_async_copy(w, dst, sems.at[i]))
    for copy in copies:
        copy.start()
    for copy in copies:
        copy.wait()
    hid = held.shape[2]
    for i, wt in enumerate((wt_left, wt_right)):
        wt[:hid] = halved_transpose(held.at[2 * i])
        wt[hid:] = halved_transpose(held.at[2 * i + 1])


def weights_call(*ws):
    chans, hid = ws[0].shape
    weights = jax.ShapeDtypeStruct((2 * hid, chans), BF16)
    square = jax.ShapeDtypeStruct((chans, hid), BF16)
    return pl.pallas_call(
        weights_kernel,
        out_shape=(weights, weights, square, square),
        in_specs=[HBM] * 6,
        out_specs=(VMEM,) * 4,
        scratch_shapes=[pltpu.VMEM((4, chans, hid), BF16), pltpu.SemaphoreType.DMA((6,))],
        compiler_params=pltpu.CompilerParams(vmem_limit_bytes=LIMIT),
        name="weights",
        cost_estimate=pl.CostEstimate(flops=10**10, bytes_accessed=1 << 20, transcendentals=0),
    )(*(pltpu.with_memory_space_constraint(w, pltpu.HBM) for w in ws))


def per_device(pair_rep, token_mask, w_a, w_a_gate, w_b, w_b_gate, w_gate, w_out):
    half, tile, chans = pair_rep.shape
    rows, cols, reps = lax.axis_size("row"), lax.axis_size("col"), lax.axis_size("rep")
    row, col, rep = lax.axis_index("row"), lax.axis_index("col"), lax.axis_index("rep")
    swap = [(p, 1 - p) for p in range(reps)]
    flat = pair_rep.reshape(-1, chans)

    near = ((0, -2, 2, 4), (-3, -5, 1, 3))
    far = ((-4, -6, 6, 8), (-1, -7, 5, 7))
    messages = first_call(flat, 8)
    chunk_rows = flat.shape[0] // 8
    got = []
    for s, message in enumerate(messages):
        pairs = [(c * cols + c, (c + near[0][s]) % rows * cols + c) for c in range(cols)]
        pairs += [(c * cols + (c + 1) % cols, (c + near[1][s]) % rows * cols + c) for c in range(cols)]
        got.append(lax.ppermute(message, ("row", "col"), pairs))
    wt_left, wt_right, w_gate, w_out = weights_call(w_a, w_a_gate, w_b, w_b_gate, w_gate, w_out)
    flat, messages = lax.optimization_barrier((flat, messages))
    x_next = lax.ppermute(flat, "col", [(c, (c - 1) % cols) for c in range(cols)])
    onward = sum((g[chunk_rows:] for g in got[1:]), got[0][chunk_rows:])
    pairs = [
        ((c + n) % rows * cols + c, (c + f) % rows * cols + c)
        for c in range(cols)
        for t in range(2)
        for n, f in zip(near[t], far[t])
    ]
    passed = lax.ppermute(onward, ("row", "col"), pairs)
    offsets = tuple(tuple(o for pair in zip(near[t], far[t]) for o in pair) for t in range(2))
    place = jnp.stack([col, (row + col) % 2]).astype(jnp.int32)

    wrapped = jnp.concatenate([token_mask, token_mask[:tile]])
    mask_k = lax.dynamic_slice_in_dim(wrapped, col * tile, 2 * tile, 0).astype(F32).reshape(1, -1)
    mask_i = lax.dynamic_slice_in_dim(token_mask, row * tile + rep * half, half, 0)
    mask_j = lax.dynamic_slice_in_dim(token_mask, col * tile + rep * half, half, 0)

    left = left_call(mask_i, pair_rep, x_next.reshape(half, tile, chans), mask_k, wt_left)
    other = lax.ppermute(left, "rep", swap)

    chunk, rest = chunk_call(got, passed)
    rest_other = lax.ppermute(rest, "row", [(r, r ^ 1) for r in range(rows)])
    gathered = lax.all_gather(chunk, "row", axis=0, tiled=False)

    right = right_call(offsets, place, mask_j, gathered, rest, rest_other, mask_k, wt_right)
    theirs = theirs_call(other, right, w_out)
    received = lax.ppermute(theirs, "rep", swap)
    ours, gate = own_call(pair_rep, w_gate, left, right, w_out)
    received = received.astype(F32)
    low = rep == 0
    projected = jnp.concatenate([jnp.where(low, ours, received), jnp.where(low, received, ours)], axis=1)
    return (gate * projected).astype(BF16)


def solution(mesh):
    placed = (P(("row", "rep"), "col", None), P(), P(), P(), P(), P(), P(), P())
    return jax.shard_map(
        per_device,
        mesh=mesh,
        in_specs=placed,
        out_specs=P(("row", "rep"), "col", None),
        check_vma=False,
    )
```

```python
import functools

import jax
import jax.numpy as jnp
from jax import lax
from jax.experimental import pallas as pl
from jax.experimental.pallas import tpu as pltpu
from jax.sharding import PartitionSpec as P

EPS = 1e-5
VMEM = pl.BlockSpec(memory_space=pltpu.VMEM)
SMEM = pl.BlockSpec(memory_space=pltpu.SMEM)
HBM = pl.BlockSpec(memory_space=pl.ANY)
F32 = jnp.float32
BF16 = jnp.bfloat16
GROUP = 16
REST = 16
LIMIT = 20 << 20


def dot(a, b, dims):
    return lax.dot_general(a, b, (dims, ((), ())), preferred_element_type=F32)


def normalise(block):
    chans = block.shape[1]
    ones = jnp.ones((chans, chans), BF16)
    centred = block.astype(F32) - dot(block, ones, ((1,), (0,))) * (1.0 / chans)
    var = dot((centred * centred).astype(BF16), ones, ((1,), (0,))) * (1.0 / chans)
    return (centred * lax.rsqrt(var + EPS)).astype(BF16)


def halved_transpose(w):
    return (w[...].astype(F32).T * 0.5).astype(BF16)


def gated(weights, normed, masks):
    hid = weights.shape[0] // 2
    both = dot(weights, normed, ((1,), (1,)))
    width = masks[0].shape[1]
    parts = []
    for n, mask in enumerate(masks):
        at = slice(n * width, (n + 1) * width)
        value = both[:hid, at] * mask
        parts.append(value + value * jnp.tanh(both[hid:, at]))
    return jnp.concatenate(parts, axis=1).reshape(hid, len(masks), width).astype(BF16)


def left_kernel(flags, x, x_next, mask_k, weights, out):
    half = x.shape[0]
    for q in range(0, half, GROUP):
        blocks = [part[i] for i in range(q, q + GROUP) for part in (x, x_next)]
        masks = [mask_k[...] * flags[i].astype(F32) for i in range(q, q + GROUP)]
        out[:, q : q + GROUP, :] = gated(weights[...], normalise(jnp.concatenate(blocks)), masks)


def left_call(flags, x, x_next, mask_k, weights):
    half, tile, chans = x.shape
    hid = weights.shape[0] // 2
    return pl.pallas_call(
        left_kernel,
        out_shape=jax.ShapeDtypeStruct((hid, half, 2 * tile), BF16),
        in_specs=[SMEM] + [VMEM] * 4,
        out_specs=VMEM,
        compiler_params=pltpu.CompilerParams(vmem_limit_bytes=LIMIT),
        name="left",
        cost_estimate=pl.CostEstimate(flops=10 * half * tile * 2 * chans * hid, bytes_accessed=2 << 20, transcendentals=4 * half * tile * hid),
    )(flags, x, x_next, mask_k, weights)


def chunk_kernel(*refs):
    *got, passed, out, rest = refs
    total = got[0][...]
    for g in got[1:]:
        total = total + g[...]
    size = (total.shape[0] - REST) // 2
    own = jnp.concatenate([total[:size], total[2 * size :]])
    normed = normalise(own + passed[...])
    out[...] = normed[: size - 1]
    rest[...] = normed[size:]


def chunk_call(got, passed):
    n, chans = passed.shape
    return pl.pallas_call(
        chunk_kernel,
        out_shape=(jax.ShapeDtypeStruct((n - REST - 1, chans), BF16), jax.ShapeDtypeStruct((REST, chans), BF16)),
        in_specs=[VMEM] * (len(got) + 1),
        out_specs=(VMEM, VMEM),
        compiler_params=pltpu.CompilerParams(vmem_limit_bytes=LIMIT),
        name="chunk",
        cost_estimate=pl.CostEstimate(flops=4 * n * chans * chans, bytes_accessed=1 << 20, transcendentals=n * chans),
    )(*got, passed)


def tri_projected(left, right, w_out, held, store):
    hid, half, _ = left.shape
    for c in range(0, hid, GROUP):
        parts = [dot(left[c + u], right[c + u], ((1,), (1,))) for u in range(GROUP)]
        held[:, c : c + GROUP, :] = jnp.swapaxes(jnp.stack(parts), 0, 1)
    pack = 128 // half
    for i in range(0, half, pack):
        tri = jnp.concatenate([held[i + u] for u in range(pack)], axis=1)
        mean = jnp.sum(tri, axis=0, keepdims=True) * (1.0 / hid)
        var = jnp.sum(tri * tri, axis=0, keepdims=True) * (1.0 / hid) - mean * mean
        normed = ((tri - mean) * lax.rsqrt(var + EPS)).astype(BF16)
        projected = dot(normed, w_out[...], ((0,), (0,)))
        for u in range(pack):
            store(i + u, projected[u * half : (u + 1) * half])


def right_kernel(offsets, place, flags, gathered, rest, rest_other, mask_k, weights, right, tiles, rests):
    shards, piece, _ = gathered.shape
    hid, half, width = right.shape
    tile = width // 2
    rests[place[1]] = rest[...].astype(F32)
    rests[1 - place[1]] = rest_other[...].astype(F32)
    whole = piece + 1 - REST
    for t in range(2):
        for s, offset in enumerate(offsets[t]):
            shard = lax.rem(place[0] + offset % shards, shards)
            at = s * (piece + 1)
            tiles[t, at : at + whole] = gathered[shard, :whole]
            last = jnp.concatenate([gathered[shard, whole:].astype(F32), rests[t, s : s + 1]])
            tiles[t, at + whole : at + whole + REST] = last.astype(BF16)
    for q in range(0, half, GROUP):
        blocks = [tiles[t, j * tile : (j + 1) * tile] for j in range(q, q + GROUP) for t in range(2)]
        masks = [mask_k[...] * flags[j].astype(F32) for j in range(q, q + GROUP)]
        right[:, q : q + GROUP, :] = gated(weights[...], jnp.concatenate(blocks), masks)


def right_call(offsets, place, flags, gathered, rest, rest_other, mask_k, weights):
    half, chans = flags.shape[0], gathered.shape[-1]
    hid, width = weights.shape[0] // 2, mask_k.shape[1]
    return pl.pallas_call(
        functools.partial(right_kernel, offsets),
        out_shape=jax.ShapeDtypeStruct((hid, half, width), BF16),
        in_specs=[SMEM] * 2 + [VMEM] * 5,
        out_specs=VMEM,
        scratch_shapes=[pltpu.VMEM((2, half * width // 2, chans), BF16), pltpu.VMEM((2, REST, chans), F32)],
        compiler_params=pltpu.CompilerParams(vmem_limit_bytes=LIMIT),
        name="right",
        cost_estimate=pl.CostEstimate(flops=5 * 10**9, bytes_accessed=4 << 20, transcendentals=half * width * hid),
    )(place, flags, gathered, rest, rest_other, mask_k, weights)


def theirs_kernel(left, right, w_out, out, held):
    def store(i, rows):
        out[i] = rows.astype(BF16)

    tri_projected(left, right, w_out, held, store)


def theirs_call(left, right, w_out):
    hid, half, _ = left.shape
    chans = w_out.shape[1]
    return pl.pallas_call(
        theirs_kernel,
        out_shape=jax.ShapeDtypeStruct((half, half, chans), BF16),
        in_specs=[VMEM] * 3,
        out_specs=VMEM,
        scratch_shapes=[pltpu.VMEM((half, hid, half), F32)],
        compiler_params=pltpu.CompilerParams(vmem_limit_bytes=LIMIT),
        name="theirs",
        cost_estimate=pl.CostEstimate(flops=8 * half * half * chans * hid, bytes_accessed=2 << 20, transcendentals=0),
    )(left, right, w_out)


def own_kernel(x, w_gate, left, right, w_out, out, gate_other, held, gate):
    half, tile, chans = x.shape
    for q in range(0, half, GROUP):
        normed = normalise(x[q : q + GROUP].reshape(GROUP * tile, chans))
        gate[q : q + GROUP] = jax.nn.sigmoid(dot(normed, w_gate[...], ((1,), (0,)))).reshape(GROUP, tile, chans)
    rep = lax.axis_index("rep")
    mine = pl.ds(pl.multiple_of(rep * half, half), half)
    gate_other[...] = gate[:, pl.ds(pl.multiple_of((1 - rep) * half, half), half), :]

    def store(i, rows):
        out[i, mine, :] = (rows * gate[i, mine, :]).astype(BF16)

    tri_projected(left, right, w_out, held, store)


def own_call(x, w_gate, left, right, w_out):
    half, tile, chans = x.shape
    hid = left.shape[0]
    return pl.pallas_call(
        own_kernel,
        out_shape=(jax.ShapeDtypeStruct((half, tile, chans), BF16), jax.ShapeDtypeStruct((half, half, chans), F32)),
        in_specs=[VMEM] * 5,
        out_specs=(VMEM, VMEM),
        scratch_shapes=[pltpu.VMEM((half, hid, half), F32), pltpu.VMEM((half, tile, chans), F32)],
        compiler_params=pltpu.CompilerParams(vmem_limit_bytes=LIMIT),
        name="own_tri",
        cost_estimate=pl.CostEstimate(flops=8 * half * tile * chans * chans, bytes_accessed=4 << 20, transcendentals=2 * half * tile * chans),
    )(x, w_gate, left, right, w_out)


def first_kernel(flat, *refs):
    *outs, tails, sems = refs
    chunks = 2 * len(outs)
    size = flat.shape[0] // chunks
    ahead = lax.axis_index("col") - lax.axis_index("row") + lax.axis_size("col")

    @pl.when(lax.rem(ahead, lax.axis_size("col")) < 2)
    def _():
        copies = []
        for s in range(chunks):
            end = (s + 1) * size
            copies.append(pltpu.make_async_copy(flat.at[end - REST : end], tails.at[s], sems.at[s]))
        for s, out in enumerate(outs):
            part = flat.at[2 * s * size : (2 * s + 2) * size]
            copies.append(pltpu.make_async_copy(part, out.at[: 2 * size], sems.at[chunks + s]))
        for copy in copies:
            copy.start()
        for copy in copies[:chunks]:
            copy.wait()
        rows = [tails[s].astype(F32)[REST - 1 :] for s in range(chunks)]
        rest = jnp.concatenate(rows + [jnp.zeros((REST - chunks, flat.shape[1]), F32)]).astype(BF16)
        for out in outs:
            out[2 * size :] = rest
        for copy in copies[chunks:]:
            copy.wait()


def first_call(flat, chunks):
    rows, chans = flat.shape
    sends = chunks // 2
    message = jax.ShapeDtypeStruct((rows // sends + REST, chans), flat.dtype)
    return pl.pallas_call(
        first_kernel,
        out_shape=(message,) * sends,
        in_specs=[HBM],
        out_specs=(VMEM,) * sends,
        scratch_shapes=[pltpu.VMEM((chunks, REST, chans), BF16), pltpu.SemaphoreType.DMA((chunks + sends,))],
        compiler_params=pltpu.CompilerParams(vmem_limit_bytes=LIMIT),
        name="first",
        cost_estimate=pl.CostEstimate(flops=0, bytes_accessed=2 << 20, transcendentals=0),
    )(pltpu.with_memory_space_constraint(flat, pltpu.HBM))


def weights_kernel(*refs):
    ws, (wt_left, wt_right, w_gate, w_out), held, sems = refs[:6], refs[6:10], refs[10], refs[11]
    copies = []
    for i, w in enumerate(ws):
        dst = (held.at[0], held.at[1], held.at[2], held.at[3], w_gate, w_out)[i]
        copies.append(pltpu.make_async_copy(w, dst, sems.at[i]))
    for copy in copies:
        copy.start()
    for copy in copies:
        copy.wait()
    hid = held.shape[2]
    for i, wt in enumerate((wt_left, wt_right)):
        wt[:hid] = halved_transpose(held.at[2 * i])
        wt[hid:] = halved_transpose(held.at[2 * i + 1])


def weights_call(*ws):
    chans, hid = ws[0].shape
    weights = jax.ShapeDtypeStruct((2 * hid, chans), BF16)
    square = jax.ShapeDtypeStruct((chans, hid), BF16)
    return pl.pallas_call(
        weights_kernel,
        out_shape=(weights, weights, square, square),
        in_specs=[HBM] * 6,
        out_specs=(VMEM,) * 4,
        scratch_shapes=[pltpu.VMEM((4, chans, hid), BF16), pltpu.SemaphoreType.DMA((6,))],
        compiler_params=pltpu.CompilerParams(vmem_limit_bytes=LIMIT),
        name="weights",
        cost_estimate=pl.CostEstimate(flops=10**10, bytes_accessed=1 << 20, transcendentals=0),
    )(*(pltpu.with_memory_space_constraint(w, pltpu.HBM) for w in ws))


def per_device(pair_rep, token_mask, w_a, w_a_gate, w_b, w_b_gate, w_gate, w_out):
    half, tile, chans = pair_rep.shape
    rows, cols, reps = lax.axis_size("row"), lax.axis_size("col"), lax.axis_size("rep")
    row, col, rep = lax.axis_index("row"), lax.axis_index("col"), lax.axis_index("rep")
    swap = [(p, 1 - p) for p in range(reps)]
    flat = pair_rep.reshape(-1, chans)

    near = ((0, -2, 2, 4), (-3, -5, 1, 3))
    far = ((-4, -6, 6, 8), (-1, -7, 5, 7))
    messages = first_call(flat, 8)
    chunk_rows = flat.shape[0] // 8
    got = []
    for s, message in enumerate(messages):
        pairs = [(c * cols + c, (c + near[0][s]) % rows * cols + c) for c in range(cols)]
        pairs += [(c * cols + (c + 1) % cols, (c + near[1][s]) % rows * cols + c) for c in range(cols)]
        got.append(lax.ppermute(message, ("row", "col"), pairs))
    wt_left, wt_right, w_gate, w_out = weights_call(w_a, w_a_gate, w_b, w_b_gate, w_gate, w_out)
    flat, messages = lax.optimization_barrier((flat, messages))
    x_next = lax.ppermute(flat, "col", [(c, (c - 1) % cols) for c in range(cols)])
    onward = sum((g[chunk_rows:] for g in got[1:]), got[0][chunk_rows:])
    pairs = [
        ((c + n) % rows * cols + c, (c + f) % rows * cols + c)
        for c in range(cols)
        for t in range(2)
        for n, f in zip(near[t], far[t])
    ]
    passed = lax.ppermute(onward, ("row", "col"), pairs)
    offsets = tuple(tuple(o for pair in zip(near[t], far[t]) for o in pair) for t in range(2))
    place = jnp.stack([col, (row + col) % 2]).astype(jnp.int32)

    wrapped = jnp.concatenate([token_mask, token_mask[:tile]])
    mask_k = lax.dynamic_slice_in_dim(wrapped, col * tile, 2 * tile, 0).astype(F32).reshape(1, -1)
    mask_i = lax.dynamic_slice_in_dim(token_mask, row * tile + rep * half, half, 0)
    mask_j = lax.dynamic_slice_in_dim(token_mask, col * tile + rep * half, half, 0)

    left = left_call(mask_i, pair_rep, x_next.reshape(half, tile, chans), mask_k, wt_left)
    other = lax.ppermute(left, "rep", swap)

    chunk, rest = chunk_call(got, passed)
    rest_other = lax.ppermute(rest, "row", [(r, r ^ 1) for r in range(rows)])
    gathered = lax.all_gather(chunk, "row", axis=0, tiled=False)

    right = right_call(offsets, place, mask_j, gathered, rest, rest_other, mask_k, wt_right)
    theirs = theirs_call(other, right, w_out)
    received = lax.ppermute(theirs, "rep", swap)
    out, gate_other = own_call(pair_rep, w_gate, left, right, w_out)
    theirs_gated = (gate_other * received.astype(F32)).astype(BF16)
    return lax.dynamic_update_slice_in_dim(out, theirs_gated, (1 - rep) * half, 1)


def solution(mesh):
    placed = (P(("row", "rep"), "col", None), P(), P(), P(), P(), P(), P(), P())
    return jax.shard_map(
        per_device,
        mesh=mesh,
        in_specs=placed,
        out_specs=P(("row", "rep"), "col", None),
        check_vma=False,
    )
```

```python
import functools

import jax
import jax.numpy as jnp
from jax import lax
from jax.experimental import pallas as pl
from jax.experimental.pallas import tpu as pltpu
from jax.sharding import PartitionSpec as P

EPS = 1e-5
VMEM = pl.BlockSpec(memory_space=pltpu.VMEM)
SMEM = pl.BlockSpec(memory_space=pltpu.SMEM)
HBM = pl.BlockSpec(memory_space=pl.ANY)
F32 = jnp.float32
BF16 = jnp.bfloat16
GROUP = 16
REST = 16
LIMIT = 20 << 20


def dot(a, b, dims):
    return lax.dot_general(a, b, (dims, ((), ())), preferred_element_type=F32)


def normalise(block):
    chans = block.shape[1]
    ones = jnp.ones((chans, chans), BF16)
    centred = block.astype(F32) - dot(block, ones, ((1,), (0,))) * (1.0 / chans)
    var = dot((centred * centred).astype(BF16), ones, ((1,), (0,))) * (1.0 / chans)
    return (centred * lax.rsqrt(var + EPS)).astype(BF16)


def halved_transpose(w):
    return (w[...].astype(F32).T * 0.5).astype(BF16)


def gated(weights, normed, masks):
    hid = weights.shape[0] // 2
    both = dot(weights, normed, ((1,), (1,)))
    width = masks[0].shape[1]
    parts = []
    for n, mask in enumerate(masks):
        at = slice(n * width, (n + 1) * width)
        value = both[:hid, at] * mask
        parts.append(value + value * jnp.tanh(both[hid:, at]))
    return jnp.concatenate(parts, axis=1).reshape(hid, len(masks), width).astype(BF16)


def left_kernel(flags, x, x_next, mask_k, weights, out):
    half = x.shape[0]
    for q in range(0, half, GROUP):
        blocks = [part[i] for i in range(q, q + GROUP) for part in (x, x_next)]
        masks = [mask_k[...] * flags[i].astype(F32) for i in range(q, q + GROUP)]
        out[:, q : q + GROUP, :] = gated(weights[...], normalise(jnp.concatenate(blocks)), masks)


def left_call(flags, x, x_next, mask_k, weights):
    half, tile, chans = x.shape
    hid = weights.shape[0] // 2
    return pl.pallas_call(
        left_kernel,
        out_shape=jax.ShapeDtypeStruct((hid, half, 2 * tile), BF16),
        in_specs=[SMEM] + [VMEM] * 4,
        out_specs=VMEM,
        compiler_params=pltpu.CompilerParams(vmem_limit_bytes=LIMIT),
        name="left",
        cost_estimate=pl.CostEstimate(flops=10 * half * tile * 2 * chans * hid, bytes_accessed=2 << 20, transcendentals=4 * half * tile * hid),
    )(flags, x, x_next, mask_k, weights)


def chunk_kernel(*refs):
    *got, passed, out, rest = refs
    total = got[0][...]
    for g in got[1:]:
        total = total + g[...]
    size = (total.shape[0] - REST) // 2
    own = jnp.concatenate([total[:size], total[2 * size :]])
    normed = normalise(own + passed[...])
    out[...] = normed[: size - 1]
    rest[...] = normed[size:]


def chunk_call(got, passed):
    n, chans = passed.shape
    return pl.pallas_call(
        chunk_kernel,
        out_shape=(jax.ShapeDtypeStruct((n - REST - 1, chans), BF16), jax.ShapeDtypeStruct((REST, chans), BF16)),
        in_specs=[VMEM] * (len(got) + 1),
        out_specs=(VMEM, VMEM),
        compiler_params=pltpu.CompilerParams(vmem_limit_bytes=LIMIT),
        name="chunk",
        cost_estimate=pl.CostEstimate(flops=4 * n * chans * chans, bytes_accessed=1 << 20, transcendentals=n * chans),
    )(*got, passed)


def tri_projected(left, right, w_out, held, store):
    hid, half, _ = left.shape
    for c in range(0, hid, GROUP):
        parts = [dot(left[c + u], right[c + u], ((1,), (1,))) for u in range(GROUP)]
        held[:, c : c + GROUP, :] = jnp.swapaxes(jnp.stack(parts), 0, 1)
    pack = 128 // half
    for i in range(0, half, pack):
        tri = jnp.concatenate([held[i + u] for u in range(pack)], axis=1)
        mean = jnp.sum(tri, axis=0, keepdims=True) * (1.0 / hid)
        var = jnp.sum(tri * tri, axis=0, keepdims=True) * (1.0 / hid) - mean * mean
        normed = ((tri - mean) * lax.rsqrt(var + EPS)).astype(BF16)
        projected = dot(normed, w_out[...], ((0,), (0,)))
        for u in range(pack):
            store(i + u, projected[u * half : (u + 1) * half])


def right_kernel(offsets, place, flags, gathered, rest, rest_other, mask_k, weights, right, tiles, rests):
    shards, piece, _ = gathered.shape
    hid, half, width = right.shape
    tile = width // 2
    rests[place[1]] = rest[...].astype(F32)
    rests[1 - place[1]] = rest_other[...].astype(F32)
    whole = piece + 1 - REST
    for t in range(2):
        for s, offset in enumerate(offsets[t]):
            shard = lax.rem(place[0] + offset % shards, shards)
            at = s * (piece + 1)
            tiles[t, at : at + whole] = gathered[shard, :whole]
            last = jnp.concatenate([gathered[shard, whole:].astype(F32), rests[t, s : s + 1]])
            tiles[t, at + whole : at + whole + REST] = last.astype(BF16)
    for q in range(0, half, GROUP):
        blocks = [tiles[t, j * tile : (j + 1) * tile] for j in range(q, q + GROUP) for t in range(2)]
        masks = [mask_k[...] * flags[j].astype(F32) for j in range(q, q + GROUP)]
        right[:, q : q + GROUP, :] = gated(weights[...], jnp.concatenate(blocks), masks)


def right_call(offsets, place, flags, gathered, rest, rest_other, mask_k, weights):
    half, chans = flags.shape[0], gathered.shape[-1]
    hid, width = weights.shape[0] // 2, mask_k.shape[1]
    return pl.pallas_call(
        functools.partial(right_kernel, offsets),
        out_shape=jax.ShapeDtypeStruct((hid, half, width), BF16),
        in_specs=[SMEM] * 2 + [VMEM] * 5,
        out_specs=VMEM,
        scratch_shapes=[pltpu.VMEM((2, half * width // 2, chans), BF16), pltpu.VMEM((2, REST, chans), F32)],
        compiler_params=pltpu.CompilerParams(vmem_limit_bytes=LIMIT),
        name="right",
        cost_estimate=pl.CostEstimate(flops=5 * 10**9, bytes_accessed=4 << 20, transcendentals=half * width * hid),
    )(place, flags, gathered, rest, rest_other, mask_k, weights)


def theirs_kernel(left, right, w_out, out, held):
    def store(i, rows):
        out[i] = rows.astype(BF16)

    tri_projected(left, right, w_out, held, store)


def theirs_call(left, right, w_out):
    hid, half, _ = left.shape
    chans = w_out.shape[1]
    return pl.pallas_call(
        theirs_kernel,
        out_shape=jax.ShapeDtypeStruct((half, half, chans), BF16),
        in_specs=[VMEM] * 3,
        out_specs=VMEM,
        scratch_shapes=[pltpu.VMEM((half, hid, half), F32)],
        compiler_params=pltpu.CompilerParams(vmem_limit_bytes=LIMIT),
        name="theirs",
        cost_estimate=pl.CostEstimate(flops=8 * half * half * chans * hid, bytes_accessed=2 << 20, transcendentals=0),
    )(left, right, w_out)


def own_kernel(x, w_gate, left, right, w_out, out, gate_other, held, gate):
    half, tile, chans = x.shape
    for q in range(0, half, GROUP):
        normed = normalise(x[q : q + GROUP].reshape(GROUP * tile, chans))
        gate[q : q + GROUP] = jax.nn.sigmoid(dot(normed, w_gate[...], ((1,), (0,)))).reshape(GROUP, tile, chans)
    rep = lax.axis_index("rep")
    mine = pl.ds(pl.multiple_of(rep * half, half), half)
    gate_other[...] = gate[:, pl.ds(pl.multiple_of((1 - rep) * half, half), half), :]

    def store(i, rows):
        out[i, mine, :] = (rows * gate[i, mine, :]).astype(BF16)

    tri_projected(left, right, w_out, held, store)


def own_call(x, w_gate, left, right, w_out):
    half, tile, chans = x.shape
    hid = left.shape[0]
    return pl.pallas_call(
        own_kernel,
        out_shape=(jax.ShapeDtypeStruct((half, tile, chans), BF16), jax.ShapeDtypeStruct((half, half, chans), F32)),
        in_specs=[VMEM] * 5,
        out_specs=(VMEM, VMEM),
        scratch_shapes=[pltpu.VMEM((half, hid, half), F32), pltpu.VMEM((half, tile, chans), F32)],
        compiler_params=pltpu.CompilerParams(vmem_limit_bytes=LIMIT),
        name="own_tri",
        cost_estimate=pl.CostEstimate(flops=8 * half * tile * chans * chans, bytes_accessed=4 << 20, transcendentals=2 * half * tile * chans),
    )(x, w_gate, left, right, w_out)


def first_kernel(flat, *refs):
    *outs, tails, sems = refs
    chunks = 2 * len(outs)
    size = flat.shape[0] // chunks
    ahead = lax.axis_index("col") - lax.axis_index("row") + lax.axis_size("col")

    @pl.when(lax.rem(ahead, lax.axis_size("col")) < 2)
    def _():
        copies = []
        for s in range(chunks):
            end = (s + 1) * size
            copies.append(pltpu.make_async_copy(flat.at[end - REST : end], tails.at[s], sems.at[s]))
        for s, out in enumerate(outs):
            part = flat.at[2 * s * size : (2 * s + 2) * size]
            copies.append(pltpu.make_async_copy(part, out.at[: 2 * size], sems.at[chunks + s]))
        for copy in copies:
            copy.start()
        for copy in copies[:chunks]:
            copy.wait()
        rows = [tails[s].astype(F32)[REST - 1 :] for s in range(chunks)]
        rest = jnp.concatenate(rows + [jnp.zeros((REST - chunks, flat.shape[1]), F32)]).astype(BF16)
        for out in outs:
            out[2 * size :] = rest
        for copy in copies[chunks:]:
            copy.wait()


def first_call(flat, chunks):
    rows, chans = flat.shape
    sends = chunks // 2
    message = jax.ShapeDtypeStruct((rows // sends + REST, chans), flat.dtype)
    return pl.pallas_call(
        first_kernel,
        out_shape=(message,) * sends,
        in_specs=[HBM],
        out_specs=(VMEM,) * sends,
        scratch_shapes=[pltpu.VMEM((chunks, REST, chans), BF16), pltpu.SemaphoreType.DMA((chunks + sends,))],
        compiler_params=pltpu.CompilerParams(vmem_limit_bytes=LIMIT),
        name="first",
        cost_estimate=pl.CostEstimate(flops=0, bytes_accessed=2 << 20, transcendentals=0),
    )(pltpu.with_memory_space_constraint(flat, pltpu.HBM))


def weights_kernel(*refs):
    ws, (wt_left, wt_right, w_gate, w_out), held, sems = refs[:6], refs[6:10], refs[10], refs[11]
    copies = []
    for i, w in enumerate(ws):
        dst = (held.at[0], held.at[1], held.at[2], held.at[3], w_gate, w_out)[i]
        copies.append(pltpu.make_async_copy(w, dst, sems.at[i]))
    for copy in copies:
        copy.start()
    for copy in copies:
        copy.wait()
    hid = held.shape[2]
    for i, wt in enumerate((wt_left, wt_right)):
        wt[:hid] = halved_transpose(held.at[2 * i])
        wt[hid:] = halved_transpose(held.at[2 * i + 1])


def weights_call(*ws):
    chans, hid = ws[0].shape
    weights = jax.ShapeDtypeStruct((2 * hid, chans), BF16)
    square = jax.ShapeDtypeStruct((chans, hid), BF16)
    return pl.pallas_call(
        weights_kernel,
        out_shape=(weights, weights, square, square),
        in_specs=[HBM] * 6,
        out_specs=(VMEM,) * 4,
        scratch_shapes=[pltpu.VMEM((4, chans, hid), BF16), pltpu.SemaphoreType.DMA((6,))],
        compiler_params=pltpu.CompilerParams(vmem_limit_bytes=LIMIT),
        name="weights",
        cost_estimate=pl.CostEstimate(flops=10**10, bytes_accessed=1 << 20, transcendentals=0),
    )(*(pltpu.with_memory_space_constraint(w, pltpu.HBM) for w in ws))


def per_device(pair_rep, token_mask, w_a, w_a_gate, w_b, w_b_gate, w_gate, w_out):
    half, tile, chans = pair_rep.shape
    rows, cols, reps = lax.axis_size("row"), lax.axis_size("col"), lax.axis_size("rep")
    row, col, rep = lax.axis_index("row"), lax.axis_index("col"), lax.axis_index("rep")
    swap = [(p, 1 - p) for p in range(reps)]
    flat = pair_rep.reshape(-1, chans)

    near = ((0, 2, 4, -2), (1, 3, -3, -5))
    far = ((-4, 6, 8, -6), (5, 7, -1, -7))
    messages = first_call(flat, 8)
    chunk_rows = flat.shape[0] // 8
    got = []
    for s, message in enumerate(messages):
        pairs = [(c * cols + c, (c + near[0][s]) % rows * cols + c) for c in range(cols)]
        pairs += [(c * cols + (c + 1) % cols, (c + near[1][s]) % rows * cols + c) for c in range(cols)]
        got.append(lax.ppermute(message, ("row", "col"), pairs))
    wt_left, wt_right, w_gate, w_out = weights_call(w_a, w_a_gate, w_b, w_b_gate, w_gate, w_out)
    flat, messages = lax.optimization_barrier((flat, messages))
    x_next = lax.ppermute(flat, "col", [(c, (c - 1) % cols) for c in range(cols)])
    onward = sum((g[chunk_rows:] for g in got[1:]), got[0][chunk_rows:])
    pairs = [
        ((c + n) % rows * cols + c, (c + f) % rows * cols + c)
        for c in range(cols)
        for t in range(2)
        for n, f in zip(near[t], far[t])
    ]
    passed = lax.ppermute(onward, ("row", "col"), pairs)
    offsets = tuple(tuple(o for pair in zip(near[t], far[t]) for o in pair) for t in range(2))
    place = jnp.stack([col, (row + col) % 2]).astype(jnp.int32)

    wrapped = jnp.concatenate([token_mask, token_mask[:tile]])
    mask_k = lax.dynamic_slice_in_dim(wrapped, col * tile, 2 * tile, 0).astype(F32).reshape(1, -1)
    mask_i = lax.dynamic_slice_in_dim(token_mask, row * tile + rep * half, half, 0)
    mask_j = lax.dynamic_slice_in_dim(token_mask, col * tile + rep * half, half, 0)

    left = left_call(mask_i, pair_rep, x_next.reshape(half, tile, chans), mask_k, wt_left)
    other = lax.ppermute(left, "rep", swap)

    chunk, rest = chunk_call(got, passed)
    rest_other = lax.ppermute(rest, "row", [(r, r ^ 1) for r in range(rows)])
    gathered = lax.all_gather(chunk, "row", axis=0, tiled=False)

    right = right_call(offsets, place, mask_j, gathered, rest, rest_other, mask_k, wt_right)
    theirs = theirs_call(other, right, w_out)
    received = lax.ppermute(theirs, "rep", swap)
    out, gate_other = own_call(pair_rep, w_gate, left, right, w_out)
    theirs_gated = (gate_other * received.astype(F32)).astype(BF16)
    return lax.dynamic_update_slice_in_dim(out, theirs_gated, (1 - rep) * half, 1)


def solution(mesh):
    placed = (P(("row", "rep"), "col", None), P(), P(), P(), P(), P(), P(), P())
    return jax.shard_map(
        per_device,
        mesh=mesh,
        in_specs=placed,
        out_specs=P(("row", "rep"), "col", None),
        check_vma=False,
    )
```

```python
import functools

import jax
import jax.numpy as jnp
from jax import lax
from jax.experimental import pallas as pl
from jax.experimental.pallas import tpu as pltpu
from jax.sharding import PartitionSpec as P

EPS = 1e-5
VMEM = pl.BlockSpec(memory_space=pltpu.VMEM)
SMEM = pl.BlockSpec(memory_space=pltpu.SMEM)
HBM = pl.BlockSpec(memory_space=pl.ANY)
F32 = jnp.float32
BF16 = jnp.bfloat16
GROUP = 16
REST = 16
LIMIT = 20 << 20


def dot(a, b, dims):
    return lax.dot_general(a, b, (dims, ((), ())), preferred_element_type=F32)


def normalise(block, exact=True):
    chans = block.shape[1]
    ones = jnp.ones((chans, chans), BF16)
    centred = block.astype(F32) - dot(block, ones, ((1,), (0,))) * (1.0 / chans)
    squares = centred * centred
    high = squares.astype(BF16)
    total = dot(high, ones, ((1,), (0,)))
    if exact:
        total = total + dot((squares - high.astype(F32)).astype(BF16), ones, ((1,), (0,)))
    var = total * (1.0 / chans)
    return (centred * lax.rsqrt(var + EPS)).astype(BF16)


def transposed(w):
    return w[...].astype(F32).T.astype(BF16)


def gated(weights, normed, masks):
    hid = weights.shape[0] // 2
    both = dot(weights, normed, ((1,), (1,)))
    width = masks[0].shape[1]
    parts = []
    for n, mask in enumerate(masks):
        at = slice(n * width, (n + 1) * width)
        parts.append(both[:hid, at] * mask * jax.nn.sigmoid(both[hid:, at]))
    return jnp.concatenate(parts, axis=1).reshape(hid, len(masks), width).astype(BF16)


def left_kernel(flags, x, x_next, mask_k, weights, out):
    half = x.shape[0]
    for q in range(0, half, GROUP):
        blocks = [part[i] for i in range(q, q + GROUP) for part in (x, x_next)]
        masks = [mask_k[...] * flags[i].astype(F32) for i in range(q, q + GROUP)]
        out[:, q : q + GROUP, :] = gated(weights[...], normalise(jnp.concatenate(blocks), exact=False), masks)


def left_call(flags, x, x_next, mask_k, weights):
    half, tile, chans = x.shape
    hid = weights.shape[0] // 2
    return pl.pallas_call(
        left_kernel,
        out_shape=jax.ShapeDtypeStruct((hid, half, 2 * tile), BF16),
        in_specs=[SMEM] + [VMEM] * 4,
        out_specs=VMEM,
        compiler_params=pltpu.CompilerParams(vmem_limit_bytes=LIMIT),
        name="left",
        cost_estimate=pl.CostEstimate(flops=10 * half * tile * 2 * chans * hid, bytes_accessed=2 << 20, transcendentals=4 * half * tile * hid),
    )(flags, x, x_next, mask_k, weights)


def chunk_kernel(*refs):
    *got, passed, out, rest = refs
    total = got[0][...]
    for g in got[1:]:
        total = total + g[...]
    size = (total.shape[0] - REST) // 2
    own = jnp.concatenate([total[:size], total[2 * size :]])
    normed = normalise(own + passed[...])
    out[...] = normed[: size - 1]
    rest[...] = normed[size:]


def chunk_call(got, passed):
    n, chans = passed.shape
    return pl.pallas_call(
        chunk_kernel,
        out_shape=(jax.ShapeDtypeStruct((n - REST - 1, chans), BF16), jax.ShapeDtypeStruct((REST, chans), BF16)),
        in_specs=[VMEM] * (len(got) + 1),
        out_specs=(VMEM, VMEM),
        compiler_params=pltpu.CompilerParams(vmem_limit_bytes=LIMIT),
        name="chunk",
        cost_estimate=pl.CostEstimate(flops=4 * n * chans * chans, bytes_accessed=1 << 20, transcendentals=n * chans),
    )(*got, passed)


def tri_projected(left, right, w_out, held, store):
    hid, half, _ = left.shape
    for c in range(0, hid, GROUP):
        parts = [dot(left[c + u], right[c + u], ((1,), (1,))) for u in range(GROUP)]
        held[:, c : c + GROUP, :] = jnp.swapaxes(jnp.stack(parts), 0, 1)
    pack = 128 // half
    for i in range(0, half, pack):
        tri = jnp.concatenate([held[i + u] for u in range(pack)], axis=1)
        mean = jnp.sum(tri, axis=0, keepdims=True) * (1.0 / hid)
        var = jnp.sum(tri * tri, axis=0, keepdims=True) * (1.0 / hid) - mean * mean
        normed = ((tri - mean) * lax.rsqrt(var + EPS)).astype(BF16)
        projected = dot(normed, w_out[...], ((0,), (0,)))
        for u in range(pack):
            store(i + u, projected[u * half : (u + 1) * half])


def right_kernel(offsets, place, flags, gathered, rest, rest_other, mask_k, weights, right, tiles, rests):
    shards, piece, _ = gathered.shape
    hid, half, width = right.shape
    tile = width // 2
    rests[place[1]] = rest[...].astype(F32)
    rests[1 - place[1]] = rest_other[...].astype(F32)
    whole = piece + 1 - REST
    for t in range(2):
        for s, offset in enumerate(offsets[t]):
            shard = lax.rem(place[0] + offset % shards, shards)
            at = s * (piece + 1)
            tiles[t, at : at + whole] = gathered[shard, :whole]
            last = jnp.concatenate([gathered[shard, whole:].astype(F32), rests[t, s : s + 1]])
            tiles[t, at + whole : at + whole + REST] = last.astype(BF16)
    for q in range(0, half, GROUP):
        blocks = [tiles[t, j * tile : (j + 1) * tile] for j in range(q, q + GROUP) for t in range(2)]
        masks = [mask_k[...] * flags[j].astype(F32) for j in range(q, q + GROUP)]
        right[:, q : q + GROUP, :] = gated(weights[...], jnp.concatenate(blocks), masks)


def right_call(offsets, place, flags, gathered, rest, rest_other, mask_k, weights):
    half, chans = flags.shape[0], gathered.shape[-1]
    hid, width = weights.shape[0] // 2, mask_k.shape[1]
    return pl.pallas_call(
        functools.partial(right_kernel, offsets),
        out_shape=jax.ShapeDtypeStruct((hid, half, width), BF16),
        in_specs=[SMEM] * 2 + [VMEM] * 5,
        out_specs=VMEM,
        scratch_shapes=[pltpu.VMEM((2, half * width // 2, chans), BF16), pltpu.VMEM((2, REST, chans), F32)],
        compiler_params=pltpu.CompilerParams(vmem_limit_bytes=LIMIT),
        name="right",
        cost_estimate=pl.CostEstimate(flops=5 * 10**9, bytes_accessed=4 << 20, transcendentals=half * width * hid),
    )(place, flags, gathered, rest, rest_other, mask_k, weights)


def theirs_kernel(left, right, w_out, out, held):
    def store(i, rows):
        out[i] = rows.astype(BF16)

    tri_projected(left, right, w_out, held, store)


def theirs_call(left, right, w_out):
    hid, half, _ = left.shape
    chans = w_out.shape[1]
    return pl.pallas_call(
        theirs_kernel,
        out_shape=jax.ShapeDtypeStruct((half, half, chans), BF16),
        in_specs=[VMEM] * 3,
        out_specs=VMEM,
        scratch_shapes=[pltpu.VMEM((half, hid, half), F32)],
        compiler_params=pltpu.CompilerParams(vmem_limit_bytes=LIMIT),
        name="theirs",
        cost_estimate=pl.CostEstimate(flops=8 * half * half * chans * hid, bytes_accessed=2 << 20, transcendentals=0),
    )(left, right, w_out)


def own_kernel(x, w_gate, left, right, w_out, out, gate_other, held, gate):
    half, tile, chans = x.shape
    for q in range(0, half, GROUP):
        normed = normalise(x[q : q + GROUP].reshape(GROUP * tile, chans))
        gate[q : q + GROUP] = jax.nn.sigmoid(dot(normed, w_gate[...], ((1,), (0,)))).reshape(GROUP, tile, chans)
    rep = lax.axis_index("rep")
    mine = pl.ds(pl.multiple_of(rep * half, half), half)
    gate_other[...] = gate[:, pl.ds(pl.multiple_of((1 - rep) * half, half), half), :]

    def store(i, rows):
        out[i, mine, :] = (rows * gate[i, mine, :]).astype(BF16)

    tri_projected(left, right, w_out, held, store)


def own_call(x, w_gate, left, right, w_out):
    half, tile, chans = x.shape
    hid = left.shape[0]
    return pl.pallas_call(
        own_kernel,
        out_shape=(jax.ShapeDtypeStruct((half, tile, chans), BF16), jax.ShapeDtypeStruct((half, half, chans), F32)),
        in_specs=[VMEM] * 5,
        out_specs=(VMEM, VMEM),
        scratch_shapes=[pltpu.VMEM((half, hid, half), F32), pltpu.VMEM((half, tile, chans), F32)],
        compiler_params=pltpu.CompilerParams(vmem_limit_bytes=LIMIT),
        name="own_tri",
        cost_estimate=pl.CostEstimate(flops=8 * half * tile * chans * chans, bytes_accessed=4 << 20, transcendentals=2 * half * tile * chans),
    )(x, w_gate, left, right, w_out)


def first_kernel(flat, *refs):
    *outs, tails, sems = refs
    chunks = 2 * len(outs)
    size = flat.shape[0] // chunks
    ahead = lax.axis_index("col") - lax.axis_index("row") + lax.axis_size("col")

    @pl.when(lax.rem(ahead, lax.axis_size("col")) < 2)
    def _():
        copies = []
        for s in range(chunks):
            end = (s + 1) * size
            copies.append(pltpu.make_async_copy(flat.at[end - REST : end], tails.at[s], sems.at[s]))
        for s, out in enumerate(outs):
            part = flat.at[2 * s * size : (2 * s + 2) * size]
            copies.append(pltpu.make_async_copy(part, out.at[: 2 * size], sems.at[chunks + s]))
        for copy in copies:
            copy.start()
        for copy in copies[:chunks]:
            copy.wait()
        rows = [tails[s].astype(F32)[REST - 1 :] for s in range(chunks)]
        rest = jnp.concatenate(rows + [jnp.zeros((REST - chunks, flat.shape[1]), F32)]).astype(BF16)
        for out in outs:
            out[2 * size :] = rest
        for copy in copies[chunks:]:
            copy.wait()


def first_call(flat, chunks):
    rows, chans = flat.shape
    sends = chunks // 2
    message = jax.ShapeDtypeStruct((rows // sends + REST, chans), flat.dtype)
    return pl.pallas_call(
        first_kernel,
        out_shape=(message,) * sends,
        in_specs=[HBM],
        out_specs=(VMEM,) * sends,
        scratch_shapes=[pltpu.VMEM((chunks, REST, chans), BF16), pltpu.SemaphoreType.DMA((chunks + sends,))],
        compiler_params=pltpu.CompilerParams(vmem_limit_bytes=LIMIT),
        name="first",
        cost_estimate=pl.CostEstimate(flops=0, bytes_accessed=2 << 20, transcendentals=0),
    )(pltpu.with_memory_space_constraint(flat, pltpu.HBM))


def weights_kernel(*refs):
    ws, (wt_left, wt_right, w_gate, w_out), held, sems = refs[:6], refs[6:10], refs[10], refs[11]
    copies = []
    for i, w in enumerate(ws):
        dst = (held.at[0], held.at[1], held.at[2], held.at[3], w_gate, w_out)[i]
        copies.append(pltpu.make_async_copy(w, dst, sems.at[i]))
    for copy in copies:
        copy.start()
    for copy in copies:
        copy.wait()
    hid = held.shape[2]
    for i, wt in enumerate((wt_left, wt_right)):
        wt[:hid] = transposed(held.at[2 * i])
        wt[hid:] = transposed(held.at[2 * i + 1])


def weights_call(*ws):
    chans, hid = ws[0].shape
    weights = jax.ShapeDtypeStruct((2 * hid, chans), BF16)
    square = jax.ShapeDtypeStruct((chans, hid), BF16)
    return pl.pallas_call(
        weights_kernel,
        out_shape=(weights, weights, square, square),
        in_specs=[HBM] * 6,
        out_specs=(VMEM,) * 4,
        scratch_shapes=[pltpu.VMEM((4, chans, hid), BF16), pltpu.SemaphoreType.DMA((6,))],
        compiler_params=pltpu.CompilerParams(vmem_limit_bytes=LIMIT),
        name="weights",
        cost_estimate=pl.CostEstimate(flops=10**10, bytes_accessed=1 << 20, transcendentals=0),
    )(*(pltpu.with_memory_space_constraint(w, pltpu.HBM) for w in ws))


def per_device(pair_rep, token_mask, w_a, w_a_gate, w_b, w_b_gate, w_gate, w_out):
    half, tile, chans = pair_rep.shape
    rows, cols, reps = lax.axis_size("row"), lax.axis_size("col"), lax.axis_size("rep")
    row, col, rep = lax.axis_index("row"), lax.axis_index("col"), lax.axis_index("rep")
    swap = [(p, 1 - p) for p in range(reps)]
    flat = pair_rep.reshape(-1, chans)

    near = ((0, 2, -2, 4), (1, 3, -3, -5))
    far = ((-4, 6, -6, 8), (5, 7, -1, -7))
    messages = first_call(flat, 8)
    chunk_rows = flat.shape[0] // 8
    got = []
    for s, message in enumerate(messages):
        pairs = [(c * cols + c, (c + near[0][s]) % rows * cols + c) for c in range(cols)]
        pairs += [(c * cols + (c + 1) % cols, (c + near[1][s]) % rows * cols + c) for c in range(cols)]
        got.append(lax.ppermute(message, ("row", "col"), pairs))
    wt_left, wt_right, w_gate, w_out = weights_call(w_a, w_a_gate, w_b, w_b_gate, w_gate, w_out)
    flat, messages = lax.optimization_barrier((flat, messages))
    x_next = lax.ppermute(flat, "col", [(c, (c - 1) % cols) for c in range(cols)])
    onward = sum((g[chunk_rows:] for g in got[1:]), got[0][chunk_rows:])
    pairs = [
        ((c + n) % rows * cols + c, (c + f) % rows * cols + c)
        for c in range(cols)
        for t in range(2)
        for n, f in zip(near[t], far[t])
    ]
    passed = lax.ppermute(onward, ("row", "col"), pairs)
    offsets = tuple(tuple(o for pair in zip(near[t], far[t]) for o in pair) for t in range(2))
    place = jnp.stack([col, (row + col) % 2]).astype(jnp.int32)

    wrapped = jnp.concatenate([token_mask, token_mask[:tile]])
    mask_k = lax.dynamic_slice_in_dim(wrapped, col * tile, 2 * tile, 0).astype(F32).reshape(1, -1)
    mask_i = lax.dynamic_slice_in_dim(token_mask, row * tile + rep * half, half, 0)
    mask_j = lax.dynamic_slice_in_dim(token_mask, col * tile + rep * half, half, 0)

    left = left_call(mask_i, pair_rep, x_next.reshape(half, tile, chans), mask_k, wt_left)
    other = lax.ppermute(left, "rep", swap)

    chunk, rest = chunk_call(got, passed)
    rest_other = lax.ppermute(rest, "row", [(r, r ^ 1) for r in range(rows)])
    gathered = lax.all_gather(chunk, "row", axis=0, tiled=False)

    right = right_call(offsets, place, mask_j, gathered, rest, rest_other, mask_k, wt_right)
    theirs = theirs_call(other, right, w_out)
    received = lax.ppermute(theirs, "rep", swap)
    out, gate_other = own_call(pair_rep, w_gate, left, right, w_out)
    theirs_gated = (gate_other * received.astype(F32)).astype(BF16)
    return lax.dynamic_update_slice_in_dim(out, theirs_gated, (1 - rep) * half, 1)


def solution(mesh):
    placed = (P(("row", "rep"), "col", None), P(), P(), P(), P(), P(), P(), P())
    return jax.shard_map(
        per_device,
        mesh=mesh,
        in_specs=placed,
        out_specs=P(("row", "rep"), "col", None),
        check_vma=False,
    )
```

```python
import functools

import jax
import jax.numpy as jnp
from jax import lax
from jax.experimental import pallas as pl
from jax.experimental.pallas import tpu as pltpu
from jax.sharding import PartitionSpec as P

EPS = 1e-5
VMEM = pl.BlockSpec(memory_space=pltpu.VMEM)
SMEM = pl.BlockSpec(memory_space=pltpu.SMEM)
HBM = pl.BlockSpec(memory_space=pl.ANY)
F32 = jnp.float32
BF16 = jnp.bfloat16
GROUP = 16
REST = 16
LIMIT = 20 << 20


def dot(a, b, dims):
    return lax.dot_general(a, b, (dims, ((), ())), preferred_element_type=F32)


def normalise(block, exact=True):
    chans = block.shape[1]
    ones = jnp.ones((chans, chans), BF16)
    centred = block.astype(F32) - dot(block, ones, ((1,), (0,))) * (1.0 / chans)
    squares = centred * centred
    high = squares.astype(BF16)
    total = dot(high, ones, ((1,), (0,)))
    if exact:
        total = total + dot((squares - high.astype(F32)).astype(BF16), ones, ((1,), (0,)))
    var = total * (1.0 / chans)
    return (centred * lax.rsqrt(var + EPS)).astype(BF16)


def transposed(w):
    return w[...].astype(F32).T.astype(BF16)


def gated(weights, normed, masks):
    hid = weights.shape[0] // 2
    both = dot(weights, normed, ((1,), (1,)))
    width = masks[0].shape[1]
    parts = []
    for n, mask in enumerate(masks):
        at = slice(n * width, (n + 1) * width)
        parts.append(both[:hid, at] * mask * jax.nn.sigmoid(both[hid:, at]))
    return jnp.concatenate(parts, axis=1).reshape(hid, len(masks), width).astype(BF16)


def left_kernel(flags, x, x_next, mask_k, weights, out):
    half = x.shape[0]
    for q in range(0, half, GROUP):
        blocks = [part[i] for i in range(q, q + GROUP) for part in (x, x_next)]
        masks = [mask_k[...] * flags[i].astype(F32) for i in range(q, q + GROUP)]
        out[:, q : q + GROUP, :] = gated(weights[...], normalise(jnp.concatenate(blocks), exact=False), masks)


def left_call(flags, x, x_next, mask_k, weights):
    half, tile, chans = x.shape
    hid = weights.shape[0] // 2
    return pl.pallas_call(
        left_kernel,
        out_shape=jax.ShapeDtypeStruct((hid, half, 2 * tile), BF16),
        in_specs=[SMEM] + [VMEM] * 4,
        out_specs=VMEM,
        compiler_params=pltpu.CompilerParams(vmem_limit_bytes=LIMIT),
        name="left",
        cost_estimate=pl.CostEstimate(flops=10 * half * tile * 2 * chans * hid, bytes_accessed=2 << 20, transcendentals=4 * half * tile * hid),
    )(flags, x, x_next, mask_k, weights)


def chunk_kernel(*refs):
    *got, passed, out, rest = refs
    total = got[0][...]
    for g in got[1:]:
        total = total + g[...]
    size = (total.shape[0] - REST) // 2
    own = jnp.concatenate([total[:size], total[2 * size :]])
    normed = normalise(own + passed[...])
    out[...] = normed[: size - 1]
    rest[...] = normed[size:]


def chunk_call(got, passed):
    n, chans = passed.shape
    return pl.pallas_call(
        chunk_kernel,
        out_shape=(jax.ShapeDtypeStruct((n - REST - 1, chans), BF16), jax.ShapeDtypeStruct((REST, chans), BF16)),
        in_specs=[VMEM] * (len(got) + 1),
        out_specs=(VMEM, VMEM),
        compiler_params=pltpu.CompilerParams(vmem_limit_bytes=LIMIT),
        name="chunk",
        cost_estimate=pl.CostEstimate(flops=4 * n * chans * chans, bytes_accessed=1 << 20, transcendentals=n * chans),
    )(*got, passed)


def tri_projected(left, right, w_out, held, store):
    hid, half, _ = left.shape
    for c in range(0, hid, GROUP):
        parts = [dot(left[c + u], right[c + u], ((1,), (1,))) for u in range(GROUP)]
        held[:, c : c + GROUP, :] = jnp.swapaxes(jnp.stack(parts), 0, 1)
    pack = 128 // half
    for i in range(0, half, pack):
        tri = jnp.concatenate([held[i + u] for u in range(pack)], axis=1)
        mean = jnp.sum(tri, axis=0, keepdims=True) * (1.0 / hid)
        var = jnp.sum(tri * tri, axis=0, keepdims=True) * (1.0 / hid) - mean * mean
        normed = ((tri - mean) * lax.rsqrt(var + EPS)).astype(BF16)
        projected = dot(normed, w_out[...], ((0,), (0,)))
        for u in range(pack):
            store(i + u, projected[u * half : (u + 1) * half])


def right_kernel(offsets, place, flags, gathered, rest, rest_other, mask_k, weights, right, tiles, rests):
    shards, piece, _ = gathered.shape
    hid, half, width = right.shape
    tile = width // 2
    rests[place[1]] = rest[...].astype(F32)
    rests[1 - place[1]] = rest_other[...].astype(F32)
    whole = piece + 1 - REST
    for t in range(2):
        for s, offset in enumerate(offsets[t]):
            shard = lax.rem(place[0] + offset % shards, shards)
            at = s * (piece + 1)
            tiles[t, at : at + whole] = gathered[shard, :whole]
            last = jnp.concatenate([gathered[shard, whole:].astype(F32), rests[t, s : s + 1]])
            tiles[t, at + whole : at + whole + REST] = last.astype(BF16)
    for q in range(0, half, GROUP):
        blocks = [tiles[t, j * tile : (j + 1) * tile] for j in range(q, q + GROUP) for t in range(2)]
        masks = [mask_k[...] * flags[j].astype(F32) for j in range(q, q + GROUP)]
        right[:, q : q + GROUP, :] = gated(weights[...], jnp.concatenate(blocks), masks)


def right_call(offsets, place, flags, gathered, rest, rest_other, mask_k, weights):
    half, chans = flags.shape[0], gathered.shape[-1]
    hid, width = weights.shape[0] // 2, mask_k.shape[1]
    return pl.pallas_call(
        functools.partial(right_kernel, offsets),
        out_shape=jax.ShapeDtypeStruct((hid, half, width), BF16),
        in_specs=[SMEM] * 2 + [VMEM] * 5,
        out_specs=VMEM,
        scratch_shapes=[pltpu.VMEM((2, half * width // 2, chans), BF16), pltpu.VMEM((2, REST, chans), F32)],
        compiler_params=pltpu.CompilerParams(vmem_limit_bytes=LIMIT),
        name="right",
        cost_estimate=pl.CostEstimate(flops=5 * 10**9, bytes_accessed=4 << 20, transcendentals=half * width * hid),
    )(place, flags, gathered, rest, rest_other, mask_k, weights)


def theirs_kernel(left, right, w_out, out, held):
    def store(i, rows):
        out[i] = rows.astype(BF16)

    tri_projected(left, right, w_out, held, store)


def theirs_call(left, right, w_out):
    hid, half, _ = left.shape
    chans = w_out.shape[1]
    return pl.pallas_call(
        theirs_kernel,
        out_shape=jax.ShapeDtypeStruct((half, half, chans), BF16),
        in_specs=[VMEM] * 3,
        out_specs=VMEM,
        scratch_shapes=[pltpu.VMEM((half, hid, half), F32)],
        compiler_params=pltpu.CompilerParams(vmem_limit_bytes=LIMIT),
        name="theirs",
        cost_estimate=pl.CostEstimate(flops=8 * half * half * chans * hid, bytes_accessed=2 << 20, transcendentals=0),
    )(left, right, w_out)


def own_kernel(x, w_gate, left, right, w_out, out, gate_other, held, gate):
    half, tile, chans = x.shape
    for q in range(0, half, GROUP):
        normed = normalise(x[q : q + GROUP].reshape(GROUP * tile, chans))
        gate[q : q + GROUP] = jax.nn.sigmoid(dot(normed, w_gate[...], ((1,), (0,)))).reshape(GROUP, tile, chans)
    rep = lax.axis_index("rep")
    mine = pl.ds(pl.multiple_of(rep * half, half), half)
    gate_other[...] = gate[:, pl.ds(pl.multiple_of((1 - rep) * half, half), half), :]

    def store(i, rows):
        out[i, mine, :] = (rows * gate[i, mine, :]).astype(BF16)

    tri_projected(left, right, w_out, held, store)


def own_call(x, w_gate, left, right, w_out):
    half, tile, chans = x.shape
    hid = left.shape[0]
    return pl.pallas_call(
        own_kernel,
        out_shape=(jax.ShapeDtypeStruct((half, tile, chans), BF16), jax.ShapeDtypeStruct((half, half, chans), F32)),
        in_specs=[VMEM] * 5,
        out_specs=(VMEM, VMEM),
        scratch_shapes=[pltpu.VMEM((half, hid, half), F32), pltpu.VMEM((half, tile, chans), F32)],
        compiler_params=pltpu.CompilerParams(vmem_limit_bytes=LIMIT),
        name="own_tri",
        cost_estimate=pl.CostEstimate(flops=8 * half * tile * chans * chans, bytes_accessed=4 << 20, transcendentals=2 * half * tile * chans),
    )(x, w_gate, left, right, w_out)


def first_kernel(flat, *refs):
    *outs, tails, sems = refs
    chunks = 2 * len(outs)
    size = flat.shape[0] // chunks
    ahead = lax.axis_index("col") - lax.axis_index("row") + lax.axis_size("col")

    @pl.when(lax.rem(ahead, lax.axis_size("col")) < 2)
    def _():
        copies = []
        for s in range(chunks):
            end = (s + 1) * size
            copies.append(pltpu.make_async_copy(flat.at[end - REST : end], tails.at[s], sems.at[s]))
        for s, out in enumerate(outs):
            part = flat.at[2 * s * size : (2 * s + 2) * size]
            copies.append(pltpu.make_async_copy(part, out.at[: 2 * size], sems.at[chunks + s]))
        for copy in copies:
            copy.start()
        for copy in copies[:chunks]:
            copy.wait()
        rows = [tails[s].astype(F32)[REST - 1 :] for s in range(chunks)]
        rest = jnp.concatenate(rows + [jnp.zeros((REST - chunks, flat.shape[1]), F32)]).astype(BF16)
        for out in outs:
            out[2 * size :] = rest
        for copy in copies[chunks:]:
            copy.wait()


def first_call(flat, chunks):
    rows, chans = flat.shape
    sends = chunks // 2
    message = jax.ShapeDtypeStruct((rows // sends + REST, chans), flat.dtype)
    return pl.pallas_call(
        first_kernel,
        out_shape=(message,) * sends,
        in_specs=[HBM],
        out_specs=(VMEM,) * sends,
        scratch_shapes=[pltpu.VMEM((chunks, REST, chans), BF16), pltpu.SemaphoreType.DMA((chunks + sends,))],
        compiler_params=pltpu.CompilerParams(vmem_limit_bytes=LIMIT),
        name="first",
        cost_estimate=pl.CostEstimate(flops=0, bytes_accessed=2 << 20, transcendentals=0),
    )(pltpu.with_memory_space_constraint(flat, pltpu.HBM))


def weights_kernel(*refs):
    ws, (wt_left, wt_right, w_gate, w_out), held, sems = refs[:6], refs[6:10], refs[10], refs[11]
    copies = []
    for i, w in enumerate(ws):
        dst = (held.at[0], held.at[1], held.at[2], held.at[3], w_gate, w_out)[i]
        copies.append(pltpu.make_async_copy(w, dst, sems.at[i]))
    for copy in copies:
        copy.start()
    for copy in copies:
        copy.wait()
    hid = held.shape[2]
    for i, wt in enumerate((wt_left, wt_right)):
        wt[:hid] = transposed(held.at[2 * i])
        wt[hid:] = transposed(held.at[2 * i + 1])


def weights_call(*ws):
    chans, hid = ws[0].shape
    weights = jax.ShapeDtypeStruct((2 * hid, chans), BF16)
    square = jax.ShapeDtypeStruct((chans, hid), BF16)
    return pl.pallas_call(
        weights_kernel,
        out_shape=(weights, weights, square, square),
        in_specs=[HBM] * 6,
        out_specs=(VMEM,) * 4,
        scratch_shapes=[pltpu.VMEM((4, chans, hid), BF16), pltpu.SemaphoreType.DMA((6,))],
        compiler_params=pltpu.CompilerParams(vmem_limit_bytes=LIMIT),
        name="weights",
        cost_estimate=pl.CostEstimate(flops=10**10, bytes_accessed=1 << 20, transcendentals=0),
    )(*(pltpu.with_memory_space_constraint(w, pltpu.HBM) for w in ws))


def per_device(pair_rep, token_mask, w_a, w_a_gate, w_b, w_b_gate, w_gate, w_out):
    half, tile, chans = pair_rep.shape
    rows, cols, reps = lax.axis_size("row"), lax.axis_size("col"), lax.axis_size("rep")
    row, col, rep = lax.axis_index("row"), lax.axis_index("col"), lax.axis_index("rep")
    swap = [(p, 1 - p) for p in range(reps)]
    flat = pair_rep.reshape(-1, chans)

    near = ((0, 2, -2, 4), (1, 3, -3, -5))
    far = ((-4, 6, -6, 8), (5, 7, -1, -7))
    messages = first_call(flat, 8)
    chunk_rows = flat.shape[0] // 8
    got = []
    for s, message in enumerate(messages):
        pairs = [(c * cols + c, (c + near[0][s]) % rows * cols + c) for c in range(cols)]
        pairs += [(c * cols + (c + 1) % cols, (c + near[1][s]) % rows * cols + c) for c in range(cols)]
        got.append(lax.ppermute(message, ("row", "col"), pairs))
    wt_left, wt_right, w_gate, w_out = weights_call(w_a, w_a_gate, w_b, w_b_gate, w_gate, w_out)
    flat, messages = lax.optimization_barrier((flat, messages))
    x_next = lax.ppermute(flat, "col", [(c, (c - 1) % cols) for c in range(cols)])
    onward = sum((g[chunk_rows:] for g in got[1:]), got[0][chunk_rows:])
    token_mask, onward = lax.optimization_barrier((token_mask, onward))
    pairs = [
        ((c + n) % rows * cols + c, (c + f) % rows * cols + c)
        for c in range(cols)
        for t in range(2)
        for n, f in zip(near[t], far[t])
    ]
    passed = lax.ppermute(onward, ("row", "col"), pairs)
    offsets = tuple(tuple(o for pair in zip(near[t], far[t]) for o in pair) for t in range(2))
    place = jnp.stack([col, (row + col) % 2]).astype(jnp.int32)

    wrapped = jnp.concatenate([token_mask, token_mask[:tile]])
    mask_k = lax.dynamic_slice_in_dim(wrapped, col * tile, 2 * tile, 0).astype(F32).reshape(1, -1)
    mask_i = lax.dynamic_slice_in_dim(token_mask, row * tile + rep * half, half, 0)
    mask_j = lax.dynamic_slice_in_dim(token_mask, col * tile + rep * half, half, 0)

    left = left_call(mask_i, pair_rep, x_next.reshape(half, tile, chans), mask_k, wt_left)
    other = lax.ppermute(left, "rep", swap)

    chunk, rest = chunk_call(got, passed)
    rest_other = lax.ppermute(rest, "row", [(r, r ^ 1) for r in range(rows)])
    gathered = lax.all_gather(chunk, "row", axis=0, tiled=False)

    right = right_call(offsets, place, mask_j, gathered, rest, rest_other, mask_k, wt_right)
    theirs = theirs_call(other, right, w_out)
    received = lax.ppermute(theirs, "rep", swap)
    out, gate_other = own_call(pair_rep, w_gate, left, right, w_out)
    theirs_gated = (gate_other * received.astype(F32)).astype(BF16)
    return lax.dynamic_update_slice_in_dim(out, theirs_gated, (1 - rep) * half, 1)


def solution(mesh):
    placed = (P(("row", "rep"), "col", None), P(), P(), P(), P(), P(), P(), P())
    return jax.shard_map(
        per_device,
        mesh=mesh,
        in_specs=placed,
        out_specs=P(("row", "rep"), "col", None),
        check_vma=False,
    )
```
